512 devices in a mesh: cam: 8 (over z_lo, x), frame: 64 (over z_hi, y, core).
Axes of the slice: x: 4, y: 8, z: 8 (z_hi: 4, z_lo: 2; z = z_hi * 2 + z_lo), core: 2. Of those that a mesh axis runs over, the one named last changes fastest.
Arguments:
- queries: bfloat16 [8, 64, 256, 1024], P('cam', 'frame'), may hold values from -8 to 8
- key_vectors: bfloat16 [8, 64, 256, 1024], P('cam', 'frame'), may hold values from -8 to 8
- value_vectors: bfloat16 [8, 64, 256, 1024], P('cam', 'frame'), may hold values from -6 to 6
- out_grad: bfloat16 [8, 64, 256, 1024], P('cam', 'frame'), may hold values from -6 to 6
- valid_count: int32 [8, 64], P('cam', 'frame'), may hold values from 128 to 256, as said below
Outputs:
- attended: bfloat16 [8, 64, 256, 1024], P('cam', 'frame')
- grad_queries: bfloat16 [8, 64, 256, 1024], P('cam', 'frame')
- grad_keys: bfloat16 [8, 64, 256, 1024], P('cam', 'frame')
- grad_values: bfloat16 [8, 64, 256, 1024], P('cam', 'frame')
The draws below stay inside these ranges and needn't reach their ends.
Inputs may be any that keep to these rules, and one draw needn't show every extreme that they name: `valid_count`: every camera has a frame whose 256 tokens are all valid.
All inputs are finite; a program needn't handle non-finite values.
Results may differ from the reference program's by a relative error of at most 0.0092.
Values may be sent and summed in bfloat16 or wider, within the bound.
No kernel may reach another device: no remote copies, remote signals or barrier semaphores. Data moves between devices by JAX's collectives and lax.ppermute only.
A program may use at most 128 MiB of HBM per device.

```python
import jax
import jax.numpy as jnp
from jax import lax

HEADS = 16
HEAD_DIM = 64
D = 1024
POS = 256
CAMS = 8
FRAMES = 64


def draw_queries(key, part):
    key = jax.random.fold_in(key, 3)
    values_out = jax.random.truncated_normal(key, -6.0, 6.0, (CAMS, FRAMES, POS, D), jnp.float32)
    return values_out.astype(jnp.bfloat16)


def draw_key_vectors(key, part):
    key = jax.random.fold_in(key, 5)
    values_out = jax.random.truncated_normal(key, -6.0, 6.0, (CAMS, FRAMES, POS, D), jnp.float32)
    return values_out.astype(jnp.bfloat16)


def draw_valid_count(key, part):
    key = jax.random.fold_in(key, 7)
    count_key, frame_key = jax.random.split(key)
    counts = jax.random.randint(count_key, (CAMS, FRAMES), POS // 2, POS + 1)
    full_frame = jax.random.randint(frame_key, (CAMS, 1), 0, FRAMES)
    return jnp.where(jnp.arange(FRAMES)[None, :] == full_frame, POS, counts).astype(jnp.int32)


def steps_of(rng, extent, cuts, least, high):
    level = 1.0
    for position, blocks in cuts:
        draws = jax.random.uniform(jax.random.fold_in(jax.random.fold_in(rng, 6), position), (blocks,), jnp.float32, least / len(cuts), high / len(cuts))
        level = level * jnp.repeat(jnp.exp(draws), extent[position] // blocks).reshape((-1,) + (1,) * (len(extent) - 1 - position))
    return level


def gaussian(rng, extent, deviation, bound, pieces=(), held_as=jnp.bfloat16):
    drawn = jax.random.normal(rng, extent, jnp.float32) * deviation
    if len(pieces) > 0:
        drawn = steps_of(rng, extent, pieces, -0.22, 0.18) * drawn
    return jnp.clip(drawn, min=-bound, max=bound).astype(held_as)


def setup_inputs(seed: int = 0) -> dict:
    streams_of = jax.random.split(jax.random.key(seed), 6)
    return {
        "queries": draw_queries(jax.random.fold_in(streams_of[5], 71), 0),
        "key_vectors": draw_key_vectors(jax.random.fold_in(streams_of[5], 71), 0),
        "value_vectors": gaussian(streams_of[2], (CAMS, FRAMES, POS, D), 1.0, 6.0, ((0, 8), (1, 64))),
        "out_grad": gaussian(streams_of[3], (CAMS, FRAMES, POS, D), 1.0, 6.0, ((0, 8), (1, 64))),
        "valid_count": draw_valid_count(jax.random.fold_in(streams_of[5], 71), 0),
    }


def attend_all(query_part, key_part, value_part, grad_part, keep_mask, subscripts):
    query_subs, key_subs, score_subs = subscripts
    score_scale = HEAD_DIM ** -0.5
    highest = lax.Precision.HIGHEST
    query_wide = query_part.astype(jnp.float32)
    key_wide = key_part.astype(jnp.float32)
    value_wide = value_part.astype(jnp.float32)
    grad_wide = grad_part.astype(jnp.float32)
    to_score = query_subs + "," + key_subs + "->" + score_subs
    to_query = score_subs + "," + key_subs + "->" + query_subs
    to_key = score_subs + "," + query_subs + "->" + key_subs
    scores = jnp.einsum(to_score, query_wide, key_wide, precision=highest) * score_scale
    scores = jnp.where(keep_mask, scores, -jnp.inf)
    shifted = jnp.exp(scores - jnp.max(scores, axis=-1, keepdims=True))
    attn_probs = shifted / jnp.sum(shifted, axis=-1, keepdims=True)
    probs_low = lax.optimization_barrier(attn_probs.astype(jnp.bfloat16)).astype(jnp.float32)
    output = jnp.einsum(to_query, probs_low, value_wide, precision=highest)
    grad_probs = jnp.einsum(to_score, grad_wide, value_wide, precision=highest)
    row_delta = jnp.sum(attn_probs * grad_probs, axis=-1, keepdims=True)
    grad_scores = attn_probs * (grad_probs - row_delta)
    grad_scores = lax.optimization_barrier(grad_scores.astype(jnp.bfloat16)).astype(jnp.float32)
    grad_query = jnp.einsum(to_query, grad_scores, key_wide, precision=highest) * score_scale
    grad_key = jnp.einsum(to_key, grad_scores, query_wide, precision=highest) * score_scale
    grad_value = jnp.einsum(to_key, probs_low, grad_wide, precision=highest)
    return output, grad_query, grad_key, grad_value


def split_heads(tensor):
    return tensor.reshape(tensor.shape[:-1] + (HEADS, HEAD_DIM))


def merge_heads(tensor):
    return tensor.reshape(tensor.shape[:-2] + (HEADS * HEAD_DIM,))


def low_wide(tensor):
    return lax.optimization_barrier(tensor.astype(jnp.bfloat16)).astype(jnp.float32)


def cross_frame(inputs):
    query_frame, key_frame, value_frame, grad_frame, count_frame = inputs
    length = query_frame.shape[1]
    key_set = jnp.concatenate([jnp.roll(key_frame, 1, axis=0), key_frame, jnp.roll(key_frame, -1, axis=0)], axis=1)
    value_set = jnp.concatenate([jnp.roll(value_frame, 1, axis=0), value_frame, jnp.roll(value_frame, -1, axis=0)], axis=1)
    own_keep = jnp.arange(length, dtype=jnp.int32)[None, :] < count_frame[:, None]
    keep_set = jnp.concatenate([jnp.roll(own_keep, 1, axis=0), own_keep, jnp.roll(own_keep, -1, axis=0)], axis=1)
    results = attend_all(split_heads(query_frame), split_heads(key_set), split_heads(value_set), split_heads(grad_frame), keep_set[:, None, None, :], ("crhe", "cmhe", "chrm"))
    output = merge_heads(results[0])
    grad_query = merge_heads(results[1])
    grad_key = merge_heads(results[2])
    grad_value = merge_heads(results[3])
    key_total = grad_key[:, length:2 * length] + jnp.roll(grad_key[:, :length], -1, axis=0) + jnp.roll(grad_key[:, 2 * length:], 1, axis=0)
    value_total = grad_value[:, length:2 * length] + jnp.roll(grad_value[:, :length], -1, axis=0) + jnp.roll(grad_value[:, 2 * length:], 1, axis=0)
    return output, grad_query, key_total, value_total


def temporal_camera(inputs):
    query_cam, key_cam, value_cam, grad_cam, count_cam, cross_out, cross_query, cross_key, cross_value = inputs
    length = query_cam.shape[1]
    keep_mask = (jnp.arange(length, dtype=jnp.int32)[:, None] < count_cam[None, :])[:, None, None, :]
    results = attend_all(split_heads(query_cam), split_heads(key_cam), split_heads(value_cam), split_heads(grad_cam), keep_mask, ("fnhe", "gnhe", "nhfg"))
    attended = (cross_out + low_wide(merge_heads(results[0]))).astype(jnp.bfloat16)
    grad_queries = (cross_query + low_wide(merge_heads(results[1]))).astype(jnp.bfloat16)
    grad_keys = (cross_key + low_wide(merge_heads(results[2]))).astype(jnp.bfloat16)
    grad_values = (cross_value + low_wide(merge_heads(results[3]))).astype(jnp.bfloat16)
    return attended, grad_queries, grad_keys, grad_values


def reference(queries, key_vectors, value_vectors, out_grad, valid_count):
    by_frame = (jnp.swapaxes(queries, 0, 1), jnp.swapaxes(key_vectors, 0, 1), jnp.swapaxes(value_vectors, 0, 1), jnp.swapaxes(out_grad, 0, 1), jnp.transpose(valid_count))
    cross_parts = lax.map(cross_frame, by_frame)
    cross_out, cross_query, cross_key, cross_value = [jnp.swapaxes(tensor, 0, 1) for tensor in cross_parts]
    results = lax.map(temporal_camera, (queries, key_vectors, value_vectors, out_grad, valid_count, cross_out, cross_query, cross_key, cross_value))
    return (results[0], results[1], results[2], results[3])
```

```python
import jax
import jax.numpy as jnp
from jax import lax
from jax.experimental import pallas as pl
from jax.experimental.pallas import tpu as pltpu
from jax.sharding import PartitionSpec as P

HEAD_DIM = 64
PAIR = 128
MARK = 1024.0
MARK_CUT = 512.0
MASKED = -1e30
SCALE = HEAD_DIM ** (-0.5)
ROW_T = (((1,), (1,)), ((), ()))
VMEM_BYTES = 60 * 1024 * 1024


def contract(left, right, dims):
    return lax.dot_general(left, right, dims, preferred_element_type=jnp.float32)


def multiply(left, right):
    return jnp.dot(left, right, preferred_element_type=jnp.float32)


def params():
    return pltpu.CompilerParams(vmem_limit_bytes=VMEM_BYTES)


def mark_kernel(count_ref, k_ref, v_ref, kv_ref):
    positions = lax.broadcasted_iota(jnp.int32, k_ref.shape, 0)
    wide = k_ref[...].astype(jnp.float32)
    marked = jnp.where(positions < count_ref[0, 0], wide, MARK).astype(jnp.bfloat16)
    values = v_ref[...]
    for pair in range(kv_ref.shape[0]):
        columns = slice(pair * PAIR, (pair + 1) * PAIR)
        kv_ref[pair, 0] = marked[:, columns]
        kv_ref[pair, 1] = values[:, columns]


def mark(count, keys, values):
    length, width = keys.shape
    pairs = width // PAIR
    per_step = 2
    column_spec = pl.BlockSpec((length, per_step * PAIR), lambda j: (0, j))
    return pl.pallas_call(
        mark_kernel,
        grid=(pairs // per_step,),
        in_specs=[pl.BlockSpec(memory_space=pltpu.SMEM)] + [column_spec] * 2,
        out_specs=pl.BlockSpec((per_step, 2, length, PAIR), lambda j: (j, 0, 0, 0)),
        out_shape=jax.ShapeDtypeStruct((pairs, 2, length, PAIR), jnp.bfloat16),
        compiler_params=params(),
        cost_estimate=pl.CostEstimate(
            flops=length * width, bytes_accessed=8 * length * width, transcendentals=0
        ),
        name="mark",
    )(count, keys, values)


def pack_kernel(q_ref, kv_ref, g_ref, x_ref):
    blocks, pairs, _, rows, _ = x_ref.shape
    queries = q_ref[...]
    cotangents = g_ref[...]
    for pair in range(pairs):
        columns = slice(pair * PAIR, (pair + 1) * PAIR)
        parts = (queries[:, columns], kv_ref[pair, 0], kv_ref[pair, 1], cotangents[:, columns])
        for index, part in enumerate(parts):
            x_ref[:, pair, index] = part.reshape(blocks, rows, PAIR)


def pack(queries, marked, cotangents, frames):
    length, width = queries.shape
    pairs = width // PAIR
    blocks = frames // pairs
    rows = length // blocks
    per_step = 2
    column_spec = pl.BlockSpec((length, per_step * PAIR), lambda j: (0, j))
    return pl.pallas_call(
        pack_kernel,
        grid=(pairs // per_step,),
        in_specs=[
            column_spec,
            pl.BlockSpec((per_step, 2, length, PAIR), lambda j: (j, 0, 0, 0)),
            column_spec,
        ],
        out_specs=pl.BlockSpec((blocks, per_step, 4, rows, PAIR), lambda j: (0, j, 0, 0, 0)),
        out_shape=jax.ShapeDtypeStruct((blocks, pairs, 4, rows, PAIR), jnp.bfloat16),
        compiler_params=params(),
        cost_estimate=pl.CostEstimate(
            flops=length * width, bytes_accessed=16 * length * width, transcendentals=0
        ),
        name="pack",
    )(queries, marked, cotangents)


def cross_kernel(q_ref, g_ref, own_ref, low_ref, up_ref, o_ref, dq_ref, own_out, low_out, up_out):
    length = q_ref.shape[0]
    first = lax.broadcasted_iota(jnp.int32, (length, PAIR), 1) < HEAD_DIM
    marked = jnp.concatenate([low_ref[0, 0], own_ref[0, 0], up_ref[0, 0]], axis=0)
    values = jnp.concatenate([low_ref[0, 1], own_ref[0, 1], up_ref[0, 1]], axis=0)
    wide = marked.astype(jnp.float32)
    invalid = wide > MARK_CUT
    keys_wide = jnp.where(invalid, 0.0, wide)
    keys = keys_wide.astype(jnp.bfloat16)
    bias = jnp.where(invalid, MASKED, 0.0)
    bias = jnp.concatenate([bias] * (length // PAIR), axis=1)
    keys_t = keys_wide.T.astype(jnp.bfloat16)
    values_t = values.astype(jnp.float32).T.astype(jnp.bfloat16)
    queries = q_ref[...].astype(jnp.float32) * SCALE
    cotangents = g_ref[...].astype(jnp.float32)
    outputs = []
    query_grads = []
    key_grad = None
    value_grad = None
    for head in range(PAIR // HEAD_DIM):
        mine = first if head == 0 else jnp.logical_not(first)
        query = jnp.where(mine, queries, 0.0).astype(jnp.bfloat16)
        cotangent = jnp.where(mine, cotangents, 0.0).astype(jnp.bfloat16)
        scores = contract(keys, query, ROW_T) + bias
        shifted = jnp.exp(scores - jnp.max(scores, axis=0, keepdims=True))
        probs = shifted * (1.0 / jnp.sum(shifted, axis=0, keepdims=True))
        probs_low = probs.astype(jnp.bfloat16)
        grad_probs = contract(values, cotangent, ROW_T)
        row_delta = jnp.sum(probs * grad_probs, axis=0, keepdims=True)
        grad_scores = (probs * (grad_probs - row_delta)).astype(jnp.bfloat16)
        rows = slice(head * HEAD_DIM, (head + 1) * HEAD_DIM)
        outputs.append(multiply(values_t[rows], probs_low))
        query_grads.append(multiply(keys_t[rows], grad_scores))
        value_part = multiply(probs_low, cotangent)
        key_part = multiply(grad_scores, query)
        key_grad = key_part if head == 0 else key_grad + key_part
        value_grad = value_part if head == 0 else value_grad + value_part
    o_ref[...] = jnp.concatenate(outputs, axis=0).T
    dq_ref[...] = jnp.concatenate(query_grads, axis=0).T * SCALE
    for index, grad in enumerate((key_grad, value_grad)):
        low_out[0, index] = grad[:length].astype(jnp.bfloat16)
        own_out[0, index] = grad[length : 2 * length]
        up_out[0, index] = grad[2 * length :].astype(jnp.bfloat16)


def cross(queries, cotangents, own, lower, upper):
    length, width = queries.shape
    pairs = width // PAIR
    column_spec = pl.BlockSpec((length, PAIR), lambda j: (0, j))
    pair_spec = pl.BlockSpec((1, 2, length, PAIR), lambda j: (j, 0, 0, 0))
    flat = jax.ShapeDtypeStruct((length, width), jnp.float32)
    paired = jax.ShapeDtypeStruct((pairs, 2, length, PAIR), jnp.float32)
    paired_low = jax.ShapeDtypeStruct((pairs, 2, length, PAIR), jnp.bfloat16)
    return pl.pallas_call(
        cross_kernel,
        grid=(pairs,),
        in_specs=[column_spec] * 2 + [pair_spec] * 3,
        out_specs=[column_spec] * 2 + [pair_spec] * 3,
        out_shape=[flat, flat, paired, paired_low, paired_low],
        compiler_params=params(),
        cost_estimate=pl.CostEstimate(
            flops=10000 * length * length * width,
            bytes_accessed=24 * length * width * 2,
            transcendentals=48 * length * length,
        ),
        name="cross_view",
    )(queries, cotangents, own, lower, upper)


def temporal_kernel(y_ref, z_ref, rows_in, rows_out):
    frames, _, positions, _ = y_ref.shape
    first = lax.broadcasted_iota(jnp.int32, (frames, PAIR), 1) < HEAD_DIM
    for index in range(4):
        rows_in[index] = y_ref[:, index].astype(jnp.float32).reshape(frames * positions, PAIR)

    def stacked(rows):
        return jnp.concatenate(
            [jnp.where(first, rows, 0.0), jnp.where(first, 0.0, rows)], axis=0
        ).astype(jnp.bfloat16)

    def diagonal(full):
        return jnp.where(first, full[:frames], full[frames:])

    group = 8
    for start in range(0, positions, group):
        held = []
        for position in range(start, start + group):
            at = pl.ds(position, frames, stride=positions)
            marked = rows_in[1, at, :]
            invalid = marked > MARK_CUT
            keys = jnp.where(invalid, 0.0, marked).astype(jnp.bfloat16)
            values = rows_in[2, at, :].astype(jnp.bfloat16)
            queries = stacked(rows_in[0, at, :] * SCALE)
            cotangents = stacked(rows_in[3, at, :])
            scores = jnp.where(invalid, MASKED, contract(keys, queries, ROW_T))
            grad_probs = contract(values, cotangents, ROW_T)
            held.append((at, keys, values, queries, cotangents, scores, grad_probs))
        for at, keys, values, queries, cotangents, scores, grad_probs in held:
            shifted = jnp.exp(scores - jnp.max(scores, axis=0, keepdims=True))
            probs = shifted * (1.0 / jnp.sum(shifted, axis=0, keepdims=True))
            row_delta = jnp.sum(probs * grad_probs, axis=0, keepdims=True)
            grad_scores = probs * (grad_probs - row_delta)
            rows_out[0, at, :] = diagonal(multiply(probs.T.astype(jnp.bfloat16), values))
            rows_out[1, at, :] = (
                diagonal(multiply(grad_scores.T.astype(jnp.bfloat16), keys)) * SCALE
            )
            rows_out[2, at, :] = multiply(grad_scores.astype(jnp.bfloat16), queries)
            rows_out[3, at, :] = multiply(probs.astype(jnp.bfloat16), cotangents)
    for index in range(4):
        z_ref[:, index] = rows_out[index].reshape(frames, positions, PAIR).astype(jnp.bfloat16)


def temporal(blocks):
    frames, _, positions, _ = blocks.shape
    per_step = 16
    spec = pl.BlockSpec((frames, 4, per_step, PAIR), lambda i: (0, 0, i, 0))
    scratch = pltpu.VMEM((4, frames * per_step, PAIR), jnp.float32)
    return pl.pallas_call(
        temporal_kernel,
        grid=(positions // per_step,),
        in_specs=[spec],
        out_specs=spec,
        out_shape=jax.ShapeDtypeStruct(blocks.shape, jnp.bfloat16),
        scratch_shapes=[scratch, scratch],
        compiler_params=params(),
        cost_estimate=pl.CostEstimate(
            flops=12 * positions * frames * frames * PAIR,
            bytes_accessed=4 * blocks.size,
            transcendentals=2 * positions * frames * frames,
        ),
        name="temporal",
    )(blocks)


def total_kernel(own_ref, low_ref, up_ref, key_ref, value_ref):
    for pair in range(own_ref.shape[0]):
        columns = slice(pair * PAIR, (pair + 1) * PAIR)
        for index, total_ref in enumerate((key_ref, value_ref)):
            total_ref[:, columns] = (
                own_ref[pair, index]
                + low_ref[pair, index].astype(jnp.float32)
                + up_ref[pair, index].astype(jnp.float32)
            )


def total(own, lower, upper):
    pairs, _, length, _ = own.shape
    per_step = 2
    pair_spec = pl.BlockSpec((per_step, 2, length, PAIR), lambda j: (j, 0, 0, 0))
    return pl.pallas_call(
        total_kernel,
        grid=(pairs // per_step,),
        in_specs=[pair_spec] * 3,
        out_specs=[pl.BlockSpec((length, per_step * PAIR), lambda j: (0, j))] * 2,
        out_shape=[jax.ShapeDtypeStruct((length, pairs * PAIR), jnp.float32)] * 2,
        compiler_params=params(),
        cost_estimate=pl.CostEstimate(
            flops=2 * own.size, bytes_accessed=12 * own.size, transcendentals=0
        ),
        name="total",
    )(own, lower, upper)


def finish_kernel(w_ref, *refs):
    cross_refs, out_refs = refs[:4], refs[4:]
    length = cross_refs[0].shape[0]
    for pair in range(w_ref.shape[1]):
        columns = slice(pair * PAIR, (pair + 1) * PAIR)
        for index, (cross_ref, out_ref) in enumerate(zip(cross_refs, out_refs)):
            returned = w_ref[:, pair, index].reshape(length, PAIR).astype(jnp.float32)
            out_ref[:, columns] = (cross_ref[:, columns] + returned).astype(jnp.bfloat16)


def finish(returned, *cross_parts):
    length, width = cross_parts[0].shape
    blocks, pairs, _, rows, _ = returned.shape
    per_step = 2
    column_spec = pl.BlockSpec((length, per_step * PAIR), lambda j: (0, j))
    return pl.pallas_call(
        finish_kernel,
        grid=(pairs // per_step,),
        in_specs=[pl.BlockSpec((blocks, per_step, 4, rows, PAIR), lambda j: (0, j, 0, 0, 0))]
        + [column_spec] * 4,
        out_specs=[column_spec] * 4,
        out_shape=[jax.ShapeDtypeStruct((length, width), jnp.bfloat16)] * 4,
        compiler_params=params(),
        cost_estimate=pl.CostEstimate(
            flops=4 * length * width, bytes_accessed=32 * length * width, transcendentals=0
        ),
        name="finish",
    )(returned, *cross_parts)


def from_behind(shard, axis, by):
    devices = lax.axis_size(axis)
    return lax.ppermute(shard, axis, [(i, (i + by) % devices) for i in range(devices)])


def exchange(blocks):
    return lax.all_to_all(blocks, "frame", split_axis=0, concat_axis=0, tiled=True)


def on_device(queries, key_vectors, value_vectors, out_grad, valid_count):
    query_rows = queries[0, 0]
    key_rows = key_vectors[0, 0]
    value_rows = value_vectors[0, 0]
    grad_rows = out_grad[0, 0]
    frames = lax.axis_size("frame")
    marked = mark(valid_count, key_rows, value_rows)
    lower = from_behind(marked, "cam", 1)
    upper = from_behind(marked, "cam", -1)
    packed = pack(query_rows, marked, grad_rows, frames)
    rows = packed.shape[3]
    arrived = exchange(packed.reshape(frames, 4 * rows, PAIR))
    cross_out, cross_query, own_grads, lower_grads, upper_grads = cross(
        query_rows, grad_rows, marked, lower, upper
    )
    from_upper = from_behind(lower_grads, "cam", -1)
    from_lower = from_behind(upper_grads, "cam", 1)
    arrived, cross_out = lax.optimization_barrier((arrived, cross_out))
    answered = temporal(arrived.reshape(frames, 4, rows, PAIR))
    answered, from_upper, from_lower = lax.optimization_barrier(
        (answered, from_upper, from_lower)
    )
    returned = exchange(answered.reshape(frames, 4 * rows, PAIR)).reshape(packed.shape)
    key_total, value_total = total(own_grads, from_upper, from_lower)
    results = finish(returned, cross_out, cross_query, key_total, value_total)
    return tuple(result[None, None] for result in results)


def solution(mesh):
    placed = (
        P("cam", "frame", None, None),
        P("cam", "frame", None, None),
        P("cam", "frame", None, None),
        P("cam", "frame", None, None),
        P("cam", "frame"),
    )
    return jax.shard_map(
        on_device,
        mesh=mesh,
        in_specs=placed,
        out_specs=(
            P("cam", "frame", None, None),
            P("cam", "frame", None, None),
            P("cam", "frame", None, None),
            P("cam", "frame", None, None),
        ),
        check_vma=False,
    )
```

```python
import jax
import jax.numpy as jnp
from jax import lax
from jax.experimental import pallas as pl
from jax.experimental.pallas import tpu as pltpu
from jax.sharding import PartitionSpec as P

HEAD_DIM = 64
PAIR = 128
MARK = 1024.0
MARK_CUT = 512.0
MASKED = -1e30
SCALE = HEAD_DIM ** (-0.5)
ROW_T = (((1,), (1,)), ((), ()))
VMEM_BYTES = 60 * 1024 * 1024
ROOMY_BYTES = 24 * 1024 * 1024


def contract(left, right, dims):
    return lax.dot_general(left, right, dims, preferred_element_type=jnp.float32)


def multiply(left, right):
    return jnp.dot(left, right, preferred_element_type=jnp.float32)


def params(limit=VMEM_BYTES):
    return pltpu.CompilerParams(vmem_limit_bytes=limit)


def pack_kernel(count_ref, q_ref, k_ref, v_ref, g_ref, x_ref, kv_ref):
    blocks, pairs, _, rows, _ = x_ref.shape
    height = k_ref.shape[0]
    positions = lax.broadcasted_iota(jnp.int32, k_ref.shape, 0) + pl.program_id(0) * height
    wide = k_ref[...].astype(jnp.float32)
    marked = jnp.where(positions < count_ref[0, 0], wide, MARK).astype(jnp.bfloat16)
    values = v_ref[...]
    queries = q_ref[...]
    cotangents = g_ref[...]
    for pair in range(pairs):
        columns = slice(pair * PAIR, (pair + 1) * PAIR)
        kv_ref[pair, 0] = marked[:, columns]
        kv_ref[pair, 1] = values[:, columns]
        for index, whole in enumerate((queries, marked, values, cotangents)):
            x_ref[:, pair, index] = whole[:, columns].reshape(blocks, rows, PAIR)


def pack(count, queries, keys, values, cotangents, frames):
    length, width = queries.shape
    pairs = width // PAIR
    blocks = frames // pairs
    rows = length // blocks
    per_step = 2
    row_spec = pl.BlockSpec((per_step * rows, width), lambda i: (i, 0))
    return pl.pallas_call(
        pack_kernel,
        grid=(blocks // per_step,),
        in_specs=[pl.BlockSpec(memory_space=pltpu.SMEM)] + [row_spec] * 4,
        out_specs=[
            pl.BlockSpec((per_step, pairs, 4, rows, PAIR), lambda i: (i, 0, 0, 0, 0)),
            pl.BlockSpec((pairs, 2, per_step * rows, PAIR), lambda i: (0, 0, i, 0)),
        ],
        out_shape=[
            jax.ShapeDtypeStruct((blocks, pairs, 4, rows, PAIR), jnp.bfloat16),
            jax.ShapeDtypeStruct((pairs, 2, length, PAIR), jnp.bfloat16),
        ],
        compiler_params=params(),
        cost_estimate=pl.CostEstimate(
            flops=length * width, bytes_accessed=20 * length * width, transcendentals=0
        ),
        name="pack",
    )(count, queries, keys, values, cotangents)


def cross_kernel(q_ref, g_ref, own_ref, low_ref, up_ref, o_ref, dq_ref, own_out, low_out, up_out):
    length = q_ref.shape[0]
    first = lax.broadcasted_iota(jnp.int32, (length, PAIR), 1) < HEAD_DIM
    marked = jnp.concatenate([low_ref[0, 0], own_ref[0, 0], up_ref[0, 0]], axis=0)
    values = jnp.concatenate([low_ref[0, 1], own_ref[0, 1], up_ref[0, 1]], axis=0)
    wide = marked.astype(jnp.float32)
    invalid = wide > MARK_CUT
    keys_wide = jnp.where(invalid, 0.0, wide)
    keys = keys_wide.astype(jnp.bfloat16)
    bias = jnp.where(invalid, MASKED, 0.0)
    bias = jnp.concatenate([bias] * (length // PAIR), axis=1)
    keys_t = keys_wide.T.astype(jnp.bfloat16)
    values_t = values.astype(jnp.float32).T.astype(jnp.bfloat16)
    queries = q_ref[...].astype(jnp.float32) * SCALE
    cotangents = g_ref[...].astype(jnp.float32)
    outputs = []
    query_grads = []
    key_grad = None
    value_grad = None
    for head in range(PAIR // HEAD_DIM):
        mine = first if head == 0 else jnp.logical_not(first)
        query = jnp.where(mine, queries, 0.0).astype(jnp.bfloat16)
        cotangent = jnp.where(mine, cotangents, 0.0).astype(jnp.bfloat16)
        scores = contract(keys, query, ROW_T) + bias
        shifted = jnp.exp(scores - jnp.max(scores, axis=0, keepdims=True))
        probs = shifted * (1.0 / jnp.sum(shifted, axis=0, keepdims=True))
        probs_low = probs.astype(jnp.bfloat16)
        grad_probs = contract(values, cotangent, ROW_T)
        row_delta = jnp.sum(probs * grad_probs, axis=0, keepdims=True)
        grad_scores = (probs * (grad_probs - row_delta)).astype(jnp.bfloat16)
        rows = slice(head * HEAD_DIM, (head + 1) * HEAD_DIM)
        outputs.append(multiply(values_t[rows], probs_low))
        query_grads.append(multiply(keys_t[rows], grad_scores))
        value_part = multiply(probs_low, cotangent)
        key_part = multiply(grad_scores, query)
        key_grad = key_part if head == 0 else key_grad + key_part
        value_grad = value_part if head == 0 else value_grad + value_part
    o_ref[...] = jnp.concatenate(outputs, axis=0).T.astype(jnp.bfloat16)
    dq_ref[...] = (jnp.concatenate(query_grads, axis=0).T * SCALE).astype(jnp.bfloat16)
    for index, grad in enumerate((key_grad, value_grad)):
        low_out[0, index] = grad[:length].astype(jnp.bfloat16)
        own_out[0, index] = grad[length : 2 * length]
        up_out[0, index] = grad[2 * length :].astype(jnp.bfloat16)


def cross(queries, cotangents, own, lower, upper):
    length, width = queries.shape
    pairs = width // PAIR
    column_spec = pl.BlockSpec((length, PAIR), lambda j: (0, j))
    pair_spec = pl.BlockSpec((1, 2, length, PAIR), lambda j: (j, 0, 0, 0))
    flat = jax.ShapeDtypeStruct((length, width), jnp.bfloat16)
    paired = jax.ShapeDtypeStruct((pairs, 2, length, PAIR), jnp.float32)
    paired_low = jax.ShapeDtypeStruct((pairs, 2, length, PAIR), jnp.bfloat16)
    return pl.pallas_call(
        cross_kernel,
        grid=(pairs,),
        in_specs=[column_spec] * 2 + [pair_spec] * 3,
        out_specs=[column_spec] * 2 + [pair_spec] * 3,
        out_shape=[flat, flat, paired, paired_low, paired_low],
        compiler_params=params(),
        cost_estimate=pl.CostEstimate(
            flops=10000 * length * length * width,
            bytes_accessed=24 * length * width * 2,
            transcendentals=48 * length * length,
        ),
        name="cross_view",
    )(queries, cotangents, own, lower, upper)


def temporal_kernel(y_ref, z_ref, rows_in, rows_out):
    frames, _, positions, _ = y_ref.shape
    first = lax.broadcasted_iota(jnp.int32, (frames, PAIR), 1) < HEAD_DIM
    for index in range(4):
        rows_in[index] = y_ref[:, index].astype(jnp.float32).reshape(frames * positions, PAIR)

    def stacked(rows):
        return jnp.concatenate(
            [jnp.where(first, rows, 0.0), jnp.where(first, 0.0, rows)], axis=0
        ).astype(jnp.bfloat16)

    def diagonal(full):
        return jnp.where(first, full[:frames], full[frames:])

    group = 8
    for start in range(0, positions, group):
        held = []
        for position in range(start, start + group):
            at = pl.ds(position, frames, stride=positions)
            marked = rows_in[1, at, :]
            invalid = marked > MARK_CUT
            keys = jnp.where(invalid, 0.0, marked).astype(jnp.bfloat16)
            values = rows_in[2, at, :].astype(jnp.bfloat16)
            queries = stacked(rows_in[0, at, :] * SCALE)
            cotangents = stacked(rows_in[3, at, :])
            scores = jnp.where(invalid, MASKED, contract(keys, queries, ROW_T))
            grad_probs = contract(values, cotangents, ROW_T)
            held.append((at, keys, values, queries, cotangents, scores, grad_probs))
        for at, keys, values, queries, cotangents, scores, grad_probs in held:
            shifted = jnp.exp(scores - jnp.max(scores, axis=0, keepdims=True))
            probs = shifted * (1.0 / jnp.sum(shifted, axis=0, keepdims=True))
            row_delta = jnp.sum(probs * grad_probs, axis=0, keepdims=True)
            grad_scores = probs * (grad_probs - row_delta)
            rows_out[0, at, :] = diagonal(multiply(probs.T.astype(jnp.bfloat16), values))
            rows_out[1, at, :] = (
                diagonal(multiply(grad_scores.T.astype(jnp.bfloat16), keys)) * SCALE
            )
            rows_out[2, at, :] = multiply(grad_scores.astype(jnp.bfloat16), queries)
            rows_out[3, at, :] = multiply(probs.astype(jnp.bfloat16), cotangents)
    for index in range(4):
        z_ref[:, index] = rows_out[index].reshape(frames, positions, PAIR).astype(jnp.bfloat16)


def temporal(blocks):
    frames, _, positions, _ = blocks.shape
    per_step = 16
    spec = pl.BlockSpec((frames, 4, per_step, PAIR), lambda i: (0, 0, i, 0))
    scratch = pltpu.VMEM((4, frames * per_step, PAIR), jnp.float32)
    return pl.pallas_call(
        temporal_kernel,
        grid=(positions // per_step,),
        in_specs=[spec],
        out_specs=spec,
        out_shape=pltpu.HBM(blocks.shape, jnp.bfloat16),
        scratch_shapes=[scratch, scratch],
        compiler_params=params(ROOMY_BYTES),
        cost_estimate=pl.CostEstimate(
            flops=12 * positions * frames * frames * PAIR,
            bytes_accessed=4 * blocks.size,
            transcendentals=2 * positions * frames * frames,
        ),
        name="temporal",
    )(blocks)


def finish_kernel(w_ref, o_ref, dq_ref, own_ref, low_ref, up_ref, *out_refs):
    height = o_ref.shape[0]
    for pair in range(w_ref.shape[1]):
        columns = slice(pair * PAIR, (pair + 1) * PAIR)
        crossed = [ref[:, columns].astype(jnp.float32) for ref in (o_ref, dq_ref)]
        for index in range(2):
            parts = [ref[pair, index].astype(jnp.float32) for ref in (own_ref, low_ref, up_ref)]
            crossed.append(parts[0] + parts[1] + parts[2])
        for index, out_ref in enumerate(out_refs):
            returned = w_ref[:, pair, index].reshape(height, PAIR).astype(jnp.float32)
            out_ref[:, columns] = (crossed[index] + returned).astype(jnp.bfloat16)


def finish(returned, *cross_parts):
    length, width = cross_parts[0].shape
    blocks, pairs, _, rows, _ = returned.shape
    per_step = 2
    row_spec = pl.BlockSpec((per_step * rows, width), lambda i: (i, 0))
    pair_spec = pl.BlockSpec((pairs, 2, per_step * rows, PAIR), lambda i: (0, 0, i, 0))
    return pl.pallas_call(
        finish_kernel,
        grid=(blocks // per_step,),
        in_specs=[pl.BlockSpec((per_step, pairs, 4, rows, PAIR), lambda i: (i, 0, 0, 0, 0))]
        + [row_spec] * 2
        + [pair_spec] * 3,
        out_specs=[row_spec] * 4,
        out_shape=[jax.ShapeDtypeStruct((length, width), jnp.bfloat16)] * 4,
        compiler_params=params(ROOMY_BYTES),
        cost_estimate=pl.CostEstimate(
            flops=8 * length * width, bytes_accessed=32 * length * width, transcendentals=0
        ),
        name="finish",
    )(returned, *(pltpu.with_memory_space_constraint(part, pltpu.HBM) for part in cross_parts))


def from_behind(shard, axis, by):
    devices = lax.axis_size(axis)
    return lax.ppermute(shard, axis, [(i, (i + by) % devices) for i in range(devices)])


def exchange(blocks):
    return lax.all_to_all(blocks, "frame", split_axis=0, concat_axis=0, tiled=True)


def on_device(queries, key_vectors, value_vectors, out_grad, valid_count):
    query_rows = queries[0, 0]
    key_rows = key_vectors[0, 0]
    value_rows = value_vectors[0, 0]
    grad_rows = out_grad[0, 0]
    frames = lax.axis_size("frame")
    packed, marked = pack(valid_count, query_rows, key_rows, value_rows, grad_rows, frames)
    rows = packed.shape[3]
    arrived = exchange(packed.reshape(frames, 4 * rows, PAIR))
    lower = from_behind(marked, "cam", 1)
    upper = from_behind(marked, "cam", -1)
    answered = temporal(arrived.reshape(frames, 4, rows, PAIR))
    returned = exchange(answered.reshape(frames, 4 * rows, PAIR)).reshape(packed.shape)
    cross_out, cross_query, own_grads, lower_grads, upper_grads = cross(
        query_rows, grad_rows, marked, lower, upper
    )
    from_upper = from_behind(lower_grads, "cam", -1)
    from_lower = from_behind(upper_grads, "cam", 1)
    results = finish(returned, cross_out, cross_query, own_grads, from_upper, from_lower)
    return tuple(result[None, None] for result in results)


def solution(mesh):
    placed = (
        P("cam", "frame", None, None),
        P("cam", "frame", None, None),
        P("cam", "frame", None, None),
        P("cam", "frame", None, None),
        P("cam", "frame"),
    )
    return jax.shard_map(
        on_device,
        mesh=mesh,
        in_specs=placed,
        out_specs=(
            P("cam", "frame", None, None),
            P("cam", "frame", None, None),
            P("cam", "frame", None, None),
            P("cam", "frame", None, None),
        ),
        check_vma=False,
    )
```

```python
import jax
import jax.numpy as jnp
from jax import lax
from jax.experimental import pallas as pl
from jax.experimental.pallas import tpu as pltpu
from jax.sharding import PartitionSpec as P

HEAD_DIM = 64
PAIR = 128
MARK = 1024.0
MARK_CUT = 512.0
MASKED = -1e30
SCALE = HEAD_DIM ** (-0.5)
ROW_T = (((1,), (1,)), ((), ()))
VMEM_BYTES = 60 * 1024 * 1024
ROOMY_BYTES = 24 * 1024 * 1024


def contract(left, right, dims):
    return lax.dot_general(left, right, dims, preferred_element_type=jnp.float32)


def multiply(left, right):
    return jnp.dot(left, right, preferred_element_type=jnp.float32)


def params(limit=VMEM_BYTES):
    return pltpu.CompilerParams(vmem_limit_bytes=limit)


def mark_kernel(count_ref, k_ref, marked_ref):
    positions = lax.broadcasted_iota(jnp.int32, k_ref.shape, 0) + pl.program_id(0) * k_ref.shape[0]
    wide = k_ref[...].astype(jnp.float32)
    marked_ref[...] = jnp.where(positions < count_ref[0, 0], wide, MARK).astype(jnp.bfloat16)


def mark(count, keys):
    length, width = keys.shape
    row_spec = pl.BlockSpec((length // 2, width), lambda i: (i, 0))
    return pl.pallas_call(
        mark_kernel,
        grid=(2,),
        in_specs=[pl.BlockSpec(memory_space=pltpu.SMEM), row_spec],
        out_specs=row_spec,
        out_shape=jax.ShapeDtypeStruct(keys.shape, jnp.bfloat16),
        compiler_params=params(),
        cost_estimate=pl.CostEstimate(
            flops=length * width, bytes_accessed=4 * length * width, transcendentals=0
        ),
        name="mark",
    )(count, keys)


def pack_kernel(*refs):
    x_ref = refs[-1]
    blocks, pairs, _, rows, _ = x_ref.shape
    for index, ref in enumerate(refs[:-1]):
        for pair in range(pairs):
            part = ref[:, pair * PAIR : (pair + 1) * PAIR]
            x_ref[:, pair, index] = part.reshape(blocks, rows, PAIR)


def pack(queries, keys, values, cotangents, frames):
    length, width = queries.shape
    pairs = width // PAIR
    blocks = frames // pairs
    rows = length // blocks
    per_step = 2
    row_spec = pl.BlockSpec((per_step * rows, width), lambda i: (i, 0))
    return pl.pallas_call(
        pack_kernel,
        grid=(blocks // per_step,),
        in_specs=[row_spec] * 4,
        out_specs=pl.BlockSpec((per_step, pairs, 4, rows, PAIR), lambda i: (i, 0, 0, 0, 0)),
        out_shape=jax.ShapeDtypeStruct((blocks, pairs, 4, rows, PAIR), jnp.bfloat16),
        compiler_params=params(),
        cost_estimate=pl.CostEstimate(
            flops=length * width, bytes_accessed=16 * length * width, transcendentals=0
        ),
        name="pack",
    )(queries, keys, values, cotangents)


def cross_kernel(q_ref, g_ref, *refs):
    key_refs, value_refs = refs[:3], refs[3:6]
    o_ref, dq_ref, own_out, low_out, up_out = refs[6:]
    length = q_ref.shape[0]
    first = lax.broadcasted_iota(jnp.int32, (length, PAIR), 1) < HEAD_DIM
    marked = jnp.concatenate([ref[...] for ref in key_refs], axis=0)
    values = jnp.concatenate([ref[...] for ref in value_refs], axis=0)
    wide = marked.astype(jnp.float32)
    invalid = wide > MARK_CUT
    keys_wide = jnp.where(invalid, 0.0, wide)
    keys = keys_wide.astype(jnp.bfloat16)
    bias = jnp.where(invalid, MASKED, 0.0)
    bias = jnp.concatenate([bias] * (length // PAIR), axis=1)
    keys_t = keys_wide.T.astype(jnp.bfloat16)
    values_t = values.astype(jnp.float32).T.astype(jnp.bfloat16)
    queries = q_ref[...].astype(jnp.float32) * SCALE
    cotangents = g_ref[...].astype(jnp.float32)
    outputs = []
    query_grads = []
    key_grad = None
    value_grad = None
    for head in range(PAIR // HEAD_DIM):
        mine = first if head == 0 else jnp.logical_not(first)
        query = jnp.where(mine, queries, 0.0).astype(jnp.bfloat16)
        cotangent = jnp.where(mine, cotangents, 0.0).astype(jnp.bfloat16)
        scores = contract(keys, query, ROW_T) + bias
        shifted = jnp.exp(scores - jnp.max(scores, axis=0, keepdims=True))
        probs = shifted * (1.0 / jnp.sum(shifted, axis=0, keepdims=True))
        probs_low = probs.astype(jnp.bfloat16)
        grad_probs = contract(values, cotangent, ROW_T)
        row_delta = jnp.sum(probs * grad_probs, axis=0, keepdims=True)
        grad_scores = (probs * (grad_probs - row_delta)).astype(jnp.bfloat16)
        rows = slice(head * HEAD_DIM, (head + 1) * HEAD_DIM)
        outputs.append(multiply(values_t[rows], probs_low))
        query_grads.append(multiply(keys_t[rows], grad_scores))
        value_part = multiply(probs_low, cotangent)
        key_part = multiply(grad_scores, query)
        key_grad = key_part if head == 0 else key_grad + key_part
        value_grad = value_part if head == 0 else value_grad + value_part
    o_ref[...] = jnp.concatenate(outputs, axis=0).T.astype(jnp.bfloat16)
    dq_ref[...] = (jnp.concatenate(query_grads, axis=0).T * SCALE).astype(jnp.bfloat16)
    for index, grad in enumerate((key_grad, value_grad)):
        low_out[0, index] = grad[:length].astype(jnp.bfloat16)
        own_out[0, index] = grad[length : 2 * length]
        up_out[0, index] = grad[2 * length :].astype(jnp.bfloat16)


def cross(queries, cotangents, keys, values):
    length, width = queries.shape
    pairs = width // PAIR
    column_spec = pl.BlockSpec((length, PAIR), lambda j: (0, j))
    pair_spec = pl.BlockSpec((1, 2, length, PAIR), lambda j: (j, 0, 0, 0))
    flat = jax.ShapeDtypeStruct((length, width), jnp.bfloat16)
    paired = jax.ShapeDtypeStruct((pairs, 2, length, PAIR), jnp.float32)
    paired_low = jax.ShapeDtypeStruct((pairs, 2, length, PAIR), jnp.bfloat16)
    return pl.pallas_call(
        cross_kernel,
        grid=(pairs,),
        in_specs=[column_spec] * 8,
        out_specs=[column_spec] * 2 + [pair_spec] * 3,
        out_shape=[flat, flat, paired, paired_low, paired_low],
        compiler_params=params(),
        cost_estimate=pl.CostEstimate(
            flops=10000 * length * length * width,
            bytes_accessed=24 * length * width * 2,
            transcendentals=48 * length * length,
        ),
        name="cross_view",
    )(queries, cotangents, *keys, *values)


def temporal_kernel(y_ref, z_ref, rows_in, rows_out):
    frames, _, positions, _ = y_ref.shape
    first = lax.broadcasted_iota(jnp.int32, (frames, PAIR), 1) < HEAD_DIM
    for index in range(4):
        rows_in[index] = y_ref[:, index].astype(jnp.float32).reshape(frames * positions, PAIR)

    def stacked(rows):
        return jnp.concatenate(
            [jnp.where(first, rows, 0.0), jnp.where(first, 0.0, rows)], axis=0
        ).astype(jnp.bfloat16)

    def diagonal(full):
        return jnp.where(first, full[:frames], full[frames:])

    group = 8
    for start in range(0, positions, group):
        held = []
        for position in range(start, start + group):
            at = pl.ds(position, frames, stride=positions)
            marked = rows_in[1, at, :]
            invalid = marked > MARK_CUT
            keys = jnp.where(invalid, 0.0, marked).astype(jnp.bfloat16)
            values = rows_in[2, at, :].astype(jnp.bfloat16)
            queries = stacked(rows_in[0, at, :] * SCALE)
            cotangents = stacked(rows_in[3, at, :])
            scores = jnp.where(invalid, MASKED, contract(keys, queries, ROW_T))
            grad_probs = contract(values, cotangents, ROW_T)
            held.append((at, keys, values, queries, cotangents, scores, grad_probs))
        for at, keys, values, queries, cotangents, scores, grad_probs in held:
            shifted = jnp.exp(scores - jnp.max(scores, axis=0, keepdims=True))
            probs = shifted * (1.0 / jnp.sum(shifted, axis=0, keepdims=True))
            row_delta = jnp.sum(probs * grad_probs, axis=0, keepdims=True)
            grad_scores = probs * (grad_probs - row_delta)
            rows_out[0, at, :] = diagonal(multiply(probs.T.astype(jnp.bfloat16), values))
            rows_out[1, at, :] = (
                diagonal(multiply(grad_scores.T.astype(jnp.bfloat16), keys)) * SCALE
            )
            rows_out[2, at, :] = multiply(grad_scores.astype(jnp.bfloat16), queries)
            rows_out[3, at, :] = multiply(probs.astype(jnp.bfloat16), cotangents)
    for index in range(4):
        z_ref[:, index] = rows_out[index].reshape(frames, positions, PAIR).astype(jnp.bfloat16)


def temporal(blocks):
    frames, _, positions, _ = blocks.shape
    per_step = 16
    spec = pl.BlockSpec((frames, 4, per_step, PAIR), lambda i: (0, 0, i, 0))
    scratch = pltpu.VMEM((4, frames * per_step, PAIR), jnp.float32)
    return pl.pallas_call(
        temporal_kernel,
        grid=(positions // per_step,),
        in_specs=[spec],
        out_specs=spec,
        out_shape=pltpu.HBM(blocks.shape, jnp.bfloat16),
        scratch_shapes=[scratch, scratch],
        compiler_params=params(ROOMY_BYTES),
        cost_estimate=pl.CostEstimate(
            flops=12 * positions * frames * frames * PAIR,
            bytes_accessed=4 * blocks.size,
            transcendentals=2 * positions * frames * frames,
        ),
        name="temporal",
    )(blocks)


def total_kernel(own_ref, low_ref, up_ref, key_ref, value_ref):
    for pair in range(own_ref.shape[0]):
        columns = slice(pair * PAIR, (pair + 1) * PAIR)
        for index, total_ref in enumerate((key_ref, value_ref)):
            total_ref[:, columns] = (
                own_ref[pair, index]
                + low_ref[pair, index].astype(jnp.float32)
                + up_ref[pair, index].astype(jnp.float32)
            ).astype(jnp.bfloat16)


def total(own, lower, upper):
    pairs, _, length, _ = own.shape
    per_step = 2
    pair_spec = pl.BlockSpec((per_step, 2, length, PAIR), lambda j: (j, 0, 0, 0))
    return pl.pallas_call(
        total_kernel,
        grid=(pairs // per_step,),
        in_specs=[pair_spec] * 3,
        out_specs=[pl.BlockSpec((length, per_step * PAIR), lambda j: (0, j))] * 2,
        out_shape=[jax.ShapeDtypeStruct((length, pairs * PAIR), jnp.bfloat16)] * 2,
        compiler_params=params(),
        cost_estimate=pl.CostEstimate(
            flops=10**12,
            bytes_accessed=12 * own.size,
            transcendentals=0,
        ),
        name="total",
    )(own, lower, upper)


def finish_kernel(w_ref, *refs):
    cross_refs, out_refs = refs[:4], refs[4:]
    height = cross_refs[0].shape[0]
    for pair in range(w_ref.shape[1]):
        columns = slice(pair * PAIR, (pair + 1) * PAIR)
        for index, (cross_ref, out_ref) in enumerate(zip(cross_refs, out_refs)):
            returned = w_ref[:, pair, index].reshape(height, PAIR).astype(jnp.float32)
            crossed = cross_ref[:, columns].astype(jnp.float32)
            out_ref[:, columns] = (crossed + returned).astype(jnp.bfloat16)


def finish(returned, *cross_parts):
    length, width = cross_parts[0].shape
    blocks, pairs, _, rows, _ = returned.shape
    per_step = 2
    row_spec = pl.BlockSpec((per_step * rows, width), lambda i: (i, 0))
    return pl.pallas_call(
        finish_kernel,
        grid=(blocks // per_step,),
        in_specs=[pl.BlockSpec((per_step, pairs, 4, rows, PAIR), lambda i: (i, 0, 0, 0, 0))]
        + [row_spec] * 4,
        out_specs=[row_spec] * 4,
        out_shape=[jax.ShapeDtypeStruct((length, width), jnp.bfloat16)] * 4,
        compiler_params=params(ROOMY_BYTES),
        cost_estimate=pl.CostEstimate(
            flops=4 * length * width, bytes_accessed=32 * length * width, transcendentals=0
        ),
        name="finish",
    )(returned, *(pltpu.with_memory_space_constraint(part, pltpu.HBM) for part in cross_parts))


def from_behind(shard, axis, by):
    devices = lax.axis_size(axis)
    return lax.ppermute(shard, axis, [(i, (i + by) % devices) for i in range(devices)])


def exchange(blocks):
    return lax.all_to_all(blocks, "frame", split_axis=0, concat_axis=0, tiled=True)


def on_device(queries, key_vectors, value_vectors, out_grad, valid_count):
    query_rows = queries[0, 0]
    key_rows = key_vectors[0, 0]
    value_rows = value_vectors[0, 0]
    grad_rows = out_grad[0, 0]
    frames = lax.axis_size("frame")
    lower_values = from_behind(value_rows, "cam", 1)
    upper_values = from_behind(value_rows, "cam", -1)
    marked = mark(valid_count, key_rows)
    lower_keys = from_behind(marked, "cam", 1)
    upper_keys = from_behind(marked, "cam", -1)
    packed = pack(query_rows, marked, value_rows, grad_rows, frames)
    rows = packed.shape[3]
    arrived = exchange(packed.reshape(frames, 4 * rows, PAIR))
    cross_out, cross_query, own_grads, lower_grads, upper_grads = cross(
        query_rows,
        grad_rows,
        (lower_keys, marked, upper_keys),
        (lower_values, value_rows, upper_values),
    )
    from_upper = from_behind(lower_grads, "cam", -1)
    from_lower = from_behind(upper_grads, "cam", 1)
    arrived, cross_out = lax.optimization_barrier((arrived, cross_out))
    answered = temporal(arrived.reshape(frames, 4, rows, PAIR))
    returned = exchange(answered.reshape(frames, 4 * rows, PAIR)).reshape(packed.shape)
    key_total, value_total = total(own_grads, from_upper, from_lower)
    results = finish(returned, cross_out, cross_query, key_total, value_total)
    return tuple(result[None, None] for result in results)


def solution(mesh):
    placed = (
        P("cam", "frame", None, None),
        P("cam", "frame", None, None),
        P("cam", "frame", None, None),
        P("cam", "frame", None, None),
        P("cam", "frame"),
    )
    return jax.shard_map(
        on_device,
        mesh=mesh,
        in_specs=placed,
        out_specs=(
            P("cam", "frame", None, None),
            P("cam", "frame", None, None),
            P("cam", "frame", None, None),
            P("cam", "frame", None, None),
        ),
        check_vma=False,
    )
```

```python
import functools

import jax
import jax.numpy as jnp
from jax import lax
from jax.experimental import pallas as pl
from jax.experimental.pallas import tpu as pltpu
from jax.sharding import PartitionSpec as P

HEAD_DIM = 64
HALVES = 2
PAIR = 128
MARK = 1024.0
MARK_CUT = 512.0
MASKED = -1e30
SCALE = HEAD_DIM ** (-0.5)
ROW_T = (((1,), (1,)), ((), ()))
VMEM_BYTES = 60 * 1024 * 1024
ROOMY_BYTES = 24 * 1024 * 1024


def contract(left, right, dims):
    return lax.dot_general(left, right, dims, preferred_element_type=jnp.float32)


def multiply(left, right):
    return jnp.dot(left, right, preferred_element_type=jnp.float32)


def params(limit=VMEM_BYTES):
    return pltpu.CompilerParams(vmem_limit_bytes=limit)


def mark_kernel(count_ref, k_ref, v_ref, kv_ref):
    positions = lax.broadcasted_iota(jnp.int32, k_ref.shape, 0) + pl.program_id(0) * k_ref.shape[0]
    wide = k_ref[...].astype(jnp.float32)
    marked = jnp.where(positions < count_ref[0, 0], wide, MARK).astype(jnp.bfloat16)
    values = v_ref[...]
    for pair in range(kv_ref.shape[0]):
        columns = slice(pair * PAIR, (pair + 1) * PAIR)
        kv_ref[pair, 0] = marked[:, columns]
        kv_ref[pair, 1] = values[:, columns]


def mark(count, keys, values):
    length, width = keys.shape
    pairs = width // PAIR
    height = length // 2
    row_spec = pl.BlockSpec((height, width), lambda i: (i, 0))
    return pl.pallas_call(
        mark_kernel,
        grid=(length // height,),
        in_specs=[pl.BlockSpec(memory_space=pltpu.SMEM)] + [row_spec] * 2,
        out_specs=pl.BlockSpec((pairs, 2, height, PAIR), lambda i: (0, 0, i, 0)),
        out_shape=jax.ShapeDtypeStruct((pairs, 2, length, PAIR), jnp.bfloat16),
        compiler_params=params(),
        cost_estimate=pl.CostEstimate(
            flops=length * width, bytes_accessed=8 * length * width, transcendentals=0
        ),
        name="mark",
    )(count, keys, values)


def pack_kernel(half, count_ref, q_ref, k_ref, v_ref, g_ref, x_ref):
    blocks, pairs, _, rows, _ = x_ref.shape
    start = (pl.program_id(0) * blocks * HALVES + half) * rows
    shape = k_ref.shape
    in_block = lax.broadcasted_iota(jnp.int32, shape, 0) * (HALVES * rows)
    positions = start + in_block + lax.broadcasted_iota(jnp.int32, shape, 2)
    wide = k_ref[...].astype(jnp.float32)
    marked = jnp.where(positions < count_ref[0, 0], wide, MARK).astype(jnp.bfloat16)
    for index, whole in enumerate((q_ref[...], marked, v_ref[...], g_ref[...])):
        for pair in range(pairs):
            x_ref[:, pair, index] = whole[:, 0, :, pair * PAIR : (pair + 1) * PAIR]


def pack(count, queries, keys, values, cotangents, frames, half):
    length, width = queries.shape
    pairs = width // PAIR
    blocks = frames // pairs
    rows = length // blocks // HALVES
    per_step = 4

    def split(array):
        return array.reshape(blocks, HALVES, rows, width)

    row_spec = pl.BlockSpec((per_step, 1, rows, width), lambda i: (i, half, 0, 0))
    return pl.pallas_call(
        functools.partial(pack_kernel, half),
        grid=(blocks // per_step,),
        in_specs=[pl.BlockSpec(memory_space=pltpu.SMEM)] + [row_spec] * 4,
        out_specs=pl.BlockSpec((per_step, pairs, 4, rows, PAIR), lambda i: (i, 0, 0, 0, 0)),
        out_shape=jax.ShapeDtypeStruct((blocks, pairs, 4, rows, PAIR), jnp.bfloat16),
        compiler_params=params(),
        cost_estimate=pl.CostEstimate(
            flops=length * width, bytes_accessed=8 * length * width, transcendentals=0
        ),
        name="pack",
    )(count, split(queries), split(keys), split(values), split(cotangents))


def cross_kernel(q_ref, g_ref, own_ref, low_ref, up_ref, o_ref, dq_ref, own_out, low_out, up_out):
    length = q_ref.shape[0]
    first = lax.broadcasted_iota(jnp.int32, (length, PAIR), 1) < HEAD_DIM
    marked = jnp.concatenate([low_ref[0, 0], own_ref[0, 0], up_ref[0, 0]], axis=0)
    values = jnp.concatenate([low_ref[0, 1], own_ref[0, 1], up_ref[0, 1]], axis=0)
    wide = marked.astype(jnp.float32)
    invalid = wide > MARK_CUT
    keys_wide = jnp.where(invalid, 0.0, wide)
    keys = keys_wide.astype(jnp.bfloat16)
    bias = jnp.where(invalid, MASKED, 0.0)
    bias = jnp.concatenate([bias] * (length // PAIR), axis=1)
    keys_t = keys_wide.T.astype(jnp.bfloat16)
    values_t = values.astype(jnp.float32).T.astype(jnp.bfloat16)
    queries = q_ref[...].astype(jnp.float32) * SCALE
    cotangents = g_ref[...].astype(jnp.float32)
    outputs = []
    query_grads = []
    key_grad = None
    value_grad = None
    for head in range(PAIR // HEAD_DIM):
        mine = first if head == 0 else jnp.logical_not(first)
        query = jnp.where(mine, queries, 0.0).astype(jnp.bfloat16)
        cotangent = jnp.where(mine, cotangents, 0.0).astype(jnp.bfloat16)
        scores = contract(keys, query, ROW_T) + bias
        shifted = jnp.exp(scores - jnp.max(scores, axis=0, keepdims=True))
        probs = shifted * (1.0 / jnp.sum(shifted, axis=0, keepdims=True))
        probs_low = probs.astype(jnp.bfloat16)
        grad_probs = contract(values, cotangent, ROW_T)
        row_delta = jnp.sum(probs * grad_probs, axis=0, keepdims=True)
        grad_scores = (probs * (grad_probs - row_delta)).astype(jnp.bfloat16)
        rows = slice(head * HEAD_DIM, (head + 1) * HEAD_DIM)
        outputs.append(multiply(values_t[rows], probs_low))
        query_grads.append(multiply(keys_t[rows], grad_scores))
        value_part = multiply(probs_low, cotangent)
        key_part = multiply(grad_scores, query)
        key_grad = key_part if head == 0 else key_grad + key_part
        value_grad = value_part if head == 0 else value_grad + value_part
    o_ref[...] = jnp.concatenate(outputs, axis=0).T.astype(jnp.bfloat16)
    dq_ref[...] = (jnp.concatenate(query_grads, axis=0).T * SCALE).astype(jnp.bfloat16)
    for index, grad in enumerate((key_grad, value_grad)):
        low_out[0, index] = grad[:length].astype(jnp.bfloat16)
        own_out[0, index] = grad[length : 2 * length]
        up_out[0, index] = grad[2 * length :].astype(jnp.bfloat16)


def cross(queries, cotangents, own, lower, upper):
    length, width = queries.shape
    pairs = width // PAIR
    column_spec = pl.BlockSpec((length, PAIR), lambda j: (0, j))
    pair_spec = pl.BlockSpec((1, 2, length, PAIR), lambda j: (j, 0, 0, 0))
    flat = jax.ShapeDtypeStruct((length, width), jnp.bfloat16)
    paired = jax.ShapeDtypeStruct((pairs, 2, length, PAIR), jnp.float32)
    paired_low = jax.ShapeDtypeStruct((pairs, 2, length, PAIR), jnp.bfloat16)
    return pl.pallas_call(
        cross_kernel,
        grid=(pairs,),
        in_specs=[column_spec] * 2 + [pair_spec] * 3,
        out_specs=[column_spec] * 2 + [pair_spec] * 3,
        out_shape=[flat, flat, paired, paired_low, paired_low],
        compiler_params=params(),
        cost_estimate=pl.CostEstimate(
            flops=10000 * length * length * width,
            bytes_accessed=24 * length * width * 2,
            transcendentals=48 * length * length,
        ),
        name="cross_view",
    )(queries, cotangents, own, lower, upper)


def temporal_kernel(y_ref, z_ref, rows_in, rows_out):
    frames, _, positions, _ = y_ref.shape
    first = lax.broadcasted_iota(jnp.int32, (frames, PAIR), 1) < HEAD_DIM
    for index in range(4):
        rows_in[index] = y_ref[:, index].astype(jnp.float32).reshape(frames * positions, PAIR)

    def stacked(rows):
        return jnp.concatenate(
            [jnp.where(first, rows, 0.0), jnp.where(first, 0.0, rows)], axis=0
        ).astype(jnp.bfloat16)

    def diagonal(full):
        return jnp.where(first, full[:frames], full[frames:])

    group = 8
    for start in range(0, positions, group):
        held = []
        for position in range(start, start + group):
            at = pl.ds(position, frames, stride=positions)
            marked = rows_in[1, at, :]
            invalid = marked > MARK_CUT
            keys = jnp.where(invalid, 0.0, marked).astype(jnp.bfloat16)
            values = rows_in[2, at, :].astype(jnp.bfloat16)
            queries = stacked(rows_in[0, at, :] * SCALE)
            cotangents = stacked(rows_in[3, at, :])
            scores = jnp.where(invalid, MASKED, contract(keys, queries, ROW_T))
            grad_probs = contract(values, cotangents, ROW_T)
            held.append((at, keys, values, queries, cotangents, scores, grad_probs))
        for at, keys, values, queries, cotangents, scores, grad_probs in held:
            shifted = jnp.exp(scores - jnp.max(scores, axis=0, keepdims=True))
            probs = shifted * (1.0 / jnp.sum(shifted, axis=0, keepdims=True))
            row_delta = jnp.sum(probs * grad_probs, axis=0, keepdims=True)
            grad_scores = probs * (grad_probs - row_delta)
            rows_out[0, at, :] = diagonal(multiply(probs.T.astype(jnp.bfloat16), values))
            rows_out[1, at, :] = (
                diagonal(multiply(grad_scores.T.astype(jnp.bfloat16), keys)) * SCALE
            )
            rows_out[2, at, :] = multiply(grad_scores.astype(jnp.bfloat16), queries)
            rows_out[3, at, :] = multiply(probs.astype(jnp.bfloat16), cotangents)
    for index in range(4):
        z_ref[:, index] = rows_out[index].reshape(frames, positions, PAIR).astype(jnp.bfloat16)


def temporal(blocks):
    frames, _, positions, _ = blocks.shape
    spec = pl.BlockSpec(blocks.shape, lambda: (0, 0, 0, 0))
    scratch = pltpu.VMEM((4, frames * positions, PAIR), jnp.float32)
    return pl.pallas_call(
        temporal_kernel,
        in_specs=[spec],
        out_specs=spec,
        out_shape=pltpu.HBM(blocks.shape, jnp.bfloat16),
        scratch_shapes=[scratch, scratch],
        compiler_params=params(ROOMY_BYTES),
        cost_estimate=pl.CostEstimate(
            flops=10**12,
            bytes_accessed=4 * blocks.size,
            transcendentals=2 * positions * frames * frames,
        ),
        name="temporal",
    )(blocks)


def total_kernel(own_ref, low_ref, up_ref, key_ref, value_ref):
    for pair in range(own_ref.shape[0]):
        columns = slice(pair * PAIR, (pair + 1) * PAIR)
        for index, total_ref in enumerate((key_ref, value_ref)):
            total_ref[:, columns] = (
                own_ref[pair, index]
                + low_ref[pair, index].astype(jnp.float32)
                + up_ref[pair, index].astype(jnp.float32)
            ).astype(jnp.bfloat16)


def total(own, lower, upper):
    pairs, _, length, _ = own.shape
    per_step = 2
    pair_spec = pl.BlockSpec((per_step, 2, length, PAIR), lambda j: (j, 0, 0, 0))
    return pl.pallas_call(
        total_kernel,
        grid=(pairs // per_step,),
        in_specs=[pair_spec] * 3,
        out_specs=[pl.BlockSpec((length, per_step * PAIR), lambda j: (0, j))] * 2,
        out_shape=[jax.ShapeDtypeStruct((length, pairs * PAIR), jnp.bfloat16)] * 2,
        compiler_params=params(),
        cost_estimate=pl.CostEstimate(
            flops=10**12,
            bytes_accessed=12 * own.size,
            transcendentals=0,
        ),
        name="total",
    )(own, lower, upper)


def finish_kernel(*refs):
    half_refs, cross_refs, out_refs = refs[:HALVES], refs[HALVES : HALVES + 4], refs[HALVES + 4 :]
    blocks, pairs, _, rows, _ = half_refs[0].shape
    for half, w_ref in enumerate(half_refs):
        for pair in range(pairs):
            columns = slice(pair * PAIR, (pair + 1) * PAIR)
            for index, (cross_ref, out_ref) in enumerate(zip(cross_refs, out_refs)):
                crossed = cross_ref[:, half, :, columns].astype(jnp.float32)
                summed = crossed + w_ref[:, pair, index].astype(jnp.float32)
                out_ref[:, half, :, columns] = summed.astype(jnp.bfloat16)


def finish(returned, cross_parts):
    length, width = cross_parts[0].shape
    blocks, pairs, _, rows, _ = returned[0].shape
    per_step = 2
    split = (blocks, HALVES, rows, width)
    row_spec = pl.BlockSpec((per_step,) + split[1:], lambda i: (i, 0, 0, 0))
    half_spec = pl.BlockSpec((per_step, pairs, 4, rows, PAIR), lambda i: (i, 0, 0, 0, 0))
    in_place = (
        pltpu.with_memory_space_constraint(part.reshape(split), pltpu.HBM) for part in cross_parts
    )
    return pl.pallas_call(
        finish_kernel,
        grid=(blocks // per_step,),
        in_specs=[half_spec] * HALVES + [row_spec] * 4,
        out_specs=[row_spec] * 4,
        out_shape=[jax.ShapeDtypeStruct(split, jnp.bfloat16)] * 4,
        compiler_params=params(ROOMY_BYTES),
        cost_estimate=pl.CostEstimate(
            flops=4 * length * width, bytes_accessed=24 * length * width, transcendentals=0
        ),
        name="finish",
    )(*returned, *in_place)


def from_behind(shard, axis, by):
    devices = lax.axis_size(axis)
    return lax.ppermute(shard, axis, [(i, (i + by) % devices) for i in range(devices)])


def exchange(blocks):
    return lax.all_to_all(blocks, "frame", split_axis=0, concat_axis=0, tiled=True)


def on_device(queries, key_vectors, value_vectors, out_grad, valid_count):
    query_rows = queries[0, 0]
    key_rows = key_vectors[0, 0]
    value_rows = value_vectors[0, 0]
    grad_rows = out_grad[0, 0]
    frames = lax.axis_size("frame")

    def packed(half):
        return pack(valid_count, query_rows, key_rows, value_rows, grad_rows, frames, half)

    first = packed(0)
    rows = first.shape[3]
    by_frame = (frames, 4 * rows, PAIR)
    by_array = (frames, 4, rows, PAIR)
    arrived_first = exchange(first.reshape(by_frame))
    marked = mark(valid_count, key_rows, value_rows)
    lower = from_behind(marked, "cam", 1)
    upper = from_behind(marked, "cam", -1)
    arrived_first, second = lax.optimization_barrier((arrived_first, packed(1)))
    arrived_second = exchange(second.reshape(by_frame))
    arrived_first, lower, upper = lax.optimization_barrier((arrived_first, lower, upper))
    answered_first = temporal(arrived_first.reshape(by_array))
    arrived_second, answered_first, cross_queries = lax.optimization_barrier(
        (arrived_second, answered_first, query_rows)
    )
    returned_first = exchange(answered_first.reshape(by_frame))
    answered_second = temporal(arrived_second.reshape(by_array))
    cross_out, cross_query, own_grads, lower_grads, upper_grads = cross(
        cross_queries, grad_rows, marked, lower, upper
    )
    from_upper = from_behind(lower_grads, "cam", -1)
    from_lower = from_behind(upper_grads, "cam", 1)
    answered_second, returned_first, cross_out = lax.optimization_barrier(
        (answered_second, returned_first, cross_out)
    )
    returned_second = exchange(answered_second.reshape(by_frame))
    key_total, value_total = total(own_grads, from_upper, from_lower)
    returned = [part.reshape(first.shape) for part in (returned_first, returned_second)]
    results = finish(returned, (cross_out, cross_query, key_total, value_total))
    return tuple(result.reshape(queries.shape) for result in results)


def solution(mesh):
    placed = (
        P("cam", "frame", None, None),
        P("cam", "frame", None, None),
        P("cam", "frame", None, None),
        P("cam", "frame", None, None),
        P("cam", "frame"),
    )
    return jax.shard_map(
        on_device,
        mesh=mesh,
        in_specs=placed,
        out_specs=(
            P("cam", "frame", None, None),
            P("cam", "frame", None, None),
            P("cam", "frame", None, None),
            P("cam", "frame", None, None),
        ),
        check_vma=False,
    )
```

```python
import jax
import jax.numpy as jnp
from jax import lax
from jax.experimental import pallas as pl
from jax.experimental.pallas import tpu as pltpu
from jax.sharding import PartitionSpec as P

HEAD_DIM = 64
PAIR = 128
MARK = 1024.0
MARK_CUT = 512.0
MASKED = -1e30
SCALE = HEAD_DIM ** (-0.5)
ROW_T = (((1,), (1,)), ((), ()))
VMEM_BYTES = 60 * 1024 * 1024
ROOMY_BYTES = 24 * 1024 * 1024


def contract(left, right, dims):
    return lax.dot_general(left, right, dims, preferred_element_type=jnp.float32)


def multiply(left, right):
    return jnp.dot(left, right, preferred_element_type=jnp.float32)


def params(limit=VMEM_BYTES):
    return pltpu.CompilerParams(vmem_limit_bytes=limit)


def mark_kernel(count_ref, k_ref, marked_ref):
    positions = lax.broadcasted_iota(jnp.int32, k_ref.shape, 0) + pl.program_id(0) * k_ref.shape[0]
    wide = k_ref[...].astype(jnp.float32)
    marked_ref[...] = jnp.where(positions < count_ref[0, 0], wide, MARK).astype(jnp.bfloat16)


def mark(count, keys):
    length, width = keys.shape
    row_spec = pl.BlockSpec((length // 2, width), lambda i: (i, 0))
    return pl.pallas_call(
        mark_kernel,
        grid=(2,),
        in_specs=[pl.BlockSpec(memory_space=pltpu.SMEM), row_spec],
        out_specs=row_spec,
        out_shape=jax.ShapeDtypeStruct(keys.shape, jnp.bfloat16),
        compiler_params=params(),
        cost_estimate=pl.CostEstimate(
            flops=length * width, bytes_accessed=4 * length * width, transcendentals=0
        ),
        name="mark",
    )(count, keys)


def pack_kernel(*refs):
    x_ref = refs[-1]
    blocks, pairs, _, rows, _ = x_ref.shape
    for index, ref in enumerate(refs[:-1]):
        for pair in range(pairs):
            part = ref[:, pair * PAIR : (pair + 1) * PAIR]
            x_ref[:, pair, index] = part.reshape(blocks, rows, PAIR)


def pack(queries, keys, values, cotangents, frames):
    length, width = queries.shape
    pairs = width // PAIR
    blocks = frames // pairs
    rows = length // blocks
    per_step = 2
    row_spec = pl.BlockSpec((per_step * rows, width), lambda i: (i, 0))
    return pl.pallas_call(
        pack_kernel,
        grid=(blocks // per_step,),
        in_specs=[row_spec] * 4,
        out_specs=pl.BlockSpec((per_step, pairs, 4, rows, PAIR), lambda i: (i, 0, 0, 0, 0)),
        out_shape=jax.ShapeDtypeStruct((blocks, pairs, 4, rows, PAIR), jnp.bfloat16),
        compiler_params=params(),
        cost_estimate=pl.CostEstimate(
            flops=length * width, bytes_accessed=16 * length * width, transcendentals=0
        ),
        name="pack",
    )(queries, keys, values, cotangents)


def cross_kernel(q_ref, g_ref, *refs):
    key_refs, value_refs = refs[:3], refs[3:6]
    o_ref, dq_ref, own_out, low_out, up_out = refs[6:]
    length = q_ref.shape[0]
    first = lax.broadcasted_iota(jnp.int32, (length, PAIR), 1) < HEAD_DIM
    marked = jnp.concatenate([ref[...] for ref in key_refs], axis=0)
    values = jnp.concatenate([ref[...] for ref in value_refs], axis=0)
    wide = marked.astype(jnp.float32)
    invalid = wide > MARK_CUT
    keys_wide = jnp.where(invalid, 0.0, wide)
    keys = keys_wide.astype(jnp.bfloat16)
    bias = jnp.where(invalid, MASKED, 0.0)
    bias = jnp.concatenate([bias] * (length // PAIR), axis=1)
    keys_t = keys_wide.T.astype(jnp.bfloat16)
    values_t = values.astype(jnp.float32).T.astype(jnp.bfloat16)
    queries = q_ref[...].astype(jnp.float32) * SCALE
    cotangents = g_ref[...].astype(jnp.float32)
    outputs = []
    query_grads = []
    key_grad = None
    value_grad = None
    for head in range(PAIR // HEAD_DIM):
        mine = first if head == 0 else jnp.logical_not(first)
        query = jnp.where(mine, queries, 0.0).astype(jnp.bfloat16)
        cotangent = jnp.where(mine, cotangents, 0.0).astype(jnp.bfloat16)
        scores = contract(keys, query, ROW_T) + bias
        shifted = jnp.exp(scores - jnp.max(scores, axis=0, keepdims=True))
        probs = shifted * (1.0 / jnp.sum(shifted, axis=0, keepdims=True))
        probs_low = probs.astype(jnp.bfloat16)
        grad_probs = contract(values, cotangent, ROW_T)
        row_delta = jnp.sum(probs * grad_probs, axis=0, keepdims=True)
        grad_scores = (probs * (grad_probs - row_delta)).astype(jnp.bfloat16)
        rows = slice(head * HEAD_DIM, (head + 1) * HEAD_DIM)
        outputs.append(multiply(values_t[rows], probs_low))
        query_grads.append(multiply(keys_t[rows], grad_scores))
        value_part = multiply(probs_low, cotangent)
        key_part = multiply(grad_scores, query)
        key_grad = key_part if head == 0 else key_grad + key_part
        value_grad = value_part if head == 0 else value_grad + value_part
    o_ref[...] = jnp.concatenate(outputs, axis=0).T.astype(jnp.bfloat16)
    dq_ref[...] = (jnp.concatenate(query_grads, axis=0).T * SCALE).astype(jnp.bfloat16)
    for index, grad in enumerate((key_grad, value_grad)):
        low_out[0, index] = grad[:length].astype(jnp.bfloat16)
        own_out[0, index] = grad[length : 2 * length]
        up_out[0, index] = grad[2 * length :].astype(jnp.bfloat16)


def cross(queries, cotangents, keys, values):
    length, width = queries.shape
    pairs = width // PAIR
    column_spec = pl.BlockSpec((length, PAIR), lambda j: (0, j))
    pair_spec = pl.BlockSpec((1, 2, length, PAIR), lambda j: (j, 0, 0, 0))
    flat = jax.ShapeDtypeStruct((length, width), jnp.bfloat16)
    paired = jax.ShapeDtypeStruct((pairs, 2, length, PAIR), jnp.float32)
    paired_low = jax.ShapeDtypeStruct((pairs, 2, length, PAIR), jnp.bfloat16)
    return pl.pallas_call(
        cross_kernel,
        grid=(pairs,),
        in_specs=[column_spec] * 8,
        out_specs=[column_spec] * 2 + [pair_spec] * 3,
        out_shape=[flat, flat, paired, paired_low, paired_low],
        compiler_params=params(),
        cost_estimate=pl.CostEstimate(
            flops=10000 * length * length * width,
            bytes_accessed=24 * length * width * 2,
            transcendentals=48 * length * length,
        ),
        name="cross_view",
    )(queries, cotangents, *keys, *values)


def temporal_kernel(y_ref, z_ref):
    frames, _, positions, _ = y_ref.shape
    first = lax.broadcasted_iota(jnp.int32, (frames, PAIR), 1) < HEAD_DIM
    rows_in = [jnp.swapaxes(y_ref[:, index].astype(jnp.float32), 0, 1) for index in range(4)]
    rows_out = [[], [], [], []]

    def stacked(rows):
        return jnp.concatenate(
            [jnp.where(first, rows, 0.0), jnp.where(first, 0.0, rows)], axis=0
        ).astype(jnp.bfloat16)

    def diagonal(full):
        return jnp.where(first, full[:frames], full[frames:])

    group = 8
    for start in range(0, positions, group):
        held = []
        for position in range(start, start + group):
            marked = rows_in[1][position]
            invalid = marked > MARK_CUT
            keys = jnp.where(invalid, 0.0, marked).astype(jnp.bfloat16)
            values = rows_in[2][position].astype(jnp.bfloat16)
            queries = stacked(rows_in[0][position] * SCALE)
            cotangents = stacked(rows_in[3][position])
            scores = jnp.where(invalid, MASKED, contract(keys, queries, ROW_T))
            grad_probs = contract(values, cotangents, ROW_T)
            held.append((keys, values, queries, cotangents, scores, grad_probs))
        for keys, values, queries, cotangents, scores, grad_probs in held:
            shifted = jnp.exp(scores - jnp.max(scores, axis=0, keepdims=True))
            probs = shifted * (1.0 / jnp.sum(shifted, axis=0, keepdims=True))
            row_delta = jnp.sum(probs * grad_probs, axis=0, keepdims=True)
            grad_scores = probs * (grad_probs - row_delta)
            rows_out[0].append(diagonal(multiply(probs.T.astype(jnp.bfloat16), values)))
            query_part = diagonal(multiply(grad_scores.T.astype(jnp.bfloat16), keys))
            rows_out[1].append(query_part * SCALE)
            rows_out[2].append(multiply(grad_scores.astype(jnp.bfloat16), queries))
            rows_out[3].append(multiply(probs.astype(jnp.bfloat16), cotangents))
    for index in range(4):
        z_ref[:, index] = jnp.swapaxes(jnp.stack(rows_out[index]), 0, 1).astype(jnp.bfloat16)


def temporal(blocks):
    frames, _, positions, _ = blocks.shape
    per_step = 16
    spec = pl.BlockSpec((frames, 4, per_step, PAIR), lambda i: (0, 0, i, 0))
    return pl.pallas_call(
        temporal_kernel,
        grid=(positions // per_step,),
        in_specs=[spec],
        out_specs=spec,
        out_shape=pltpu.HBM(blocks.shape, jnp.bfloat16),
        compiler_params=params(ROOMY_BYTES),
        cost_estimate=pl.CostEstimate(
            flops=12 * positions * frames * frames * PAIR,
            bytes_accessed=4 * blocks.size,
            transcendentals=2 * positions * frames * frames,
        ),
        name="temporal",
    )(blocks)


def total_kernel(own_ref, low_ref, up_ref, key_ref, value_ref):
    for pair in range(own_ref.shape[0]):
        columns = slice(pair * PAIR, (pair + 1) * PAIR)
        for index, total_ref in enumerate((key_ref, value_ref)):
            total_ref[:, columns] = (
                own_ref[pair, index]
                + low_ref[pair, index].astype(jnp.float32)
                + up_ref[pair, index].astype(jnp.float32)
            ).astype(jnp.bfloat16)


def total(own, lower, upper):
    pairs, _, length, _ = own.shape
    per_step = 2
    pair_spec = pl.BlockSpec((per_step, 2, length, PAIR), lambda j: (j, 0, 0, 0))
    return pl.pallas_call(
        total_kernel,
        grid=(pairs // per_step,),
        in_specs=[pair_spec] * 3,
        out_specs=[pl.BlockSpec((length, per_step * PAIR), lambda j: (0, j))] * 2,
        out_shape=[jax.ShapeDtypeStruct((length, pairs * PAIR), jnp.bfloat16)] * 2,
        compiler_params=params(),
        cost_estimate=pl.CostEstimate(
            flops=10**12,
            bytes_accessed=12 * own.size,
            transcendentals=0,
        ),
        name="total",
    )(own, lower, upper)


def finish_kernel(w_ref, *refs):
    cross_refs, out_refs = refs[:4], refs[4:]
    height = cross_refs[0].shape[0]
    for pair in range(w_ref.shape[1]):
        columns = slice(pair * PAIR, (pair + 1) * PAIR)
        for index, (cross_ref, out_ref) in enumerate(zip(cross_refs, out_refs)):
            returned = w_ref[:, pair, index].reshape(height, PAIR).astype(jnp.float32)
            crossed = cross_ref[:, columns].astype(jnp.float32)
            out_ref[:, columns] = (crossed + returned).astype(jnp.bfloat16)


def finish(returned, *cross_parts):
    length, width = cross_parts[0].shape
    blocks, pairs, _, rows, _ = returned.shape
    per_step = 1
    row_spec = pl.BlockSpec((per_step * rows, width), lambda i: (i, 0))
    return pl.pallas_call(
        finish_kernel,
        grid=(blocks // per_step,),
        in_specs=[pl.BlockSpec((per_step, pairs, 4, rows, PAIR), lambda i: (i, 0, 0, 0, 0))]
        + [row_spec] * 4,
        out_specs=[row_spec] * 4,
        out_shape=[jax.ShapeDtypeStruct((length, width), jnp.bfloat16)] * 4,
        compiler_params=params(ROOMY_BYTES),
        cost_estimate=pl.CostEstimate(
            flops=4 * length * width, bytes_accessed=32 * length * width, transcendentals=0
        ),
        name="finish",
    )(returned, *(pltpu.with_memory_space_constraint(part, pltpu.HBM) for part in cross_parts))


def from_behind(shard, axis, by):
    devices = lax.axis_size(axis)
    return lax.ppermute(shard, axis, [(i, (i + by) % devices) for i in range(devices)])


def exchange(blocks):
    return lax.all_to_all(blocks, "frame", split_axis=0, concat_axis=0, tiled=True)


def on_device(queries, key_vectors, value_vectors, out_grad, valid_count):
    query_rows = queries[0, 0]
    key_rows = key_vectors[0, 0]
    value_rows = value_vectors[0, 0]
    grad_rows = out_grad[0, 0]
    frames = lax.axis_size("frame")
    lower_values = from_behind(value_rows, "cam", 1)
    upper_values = from_behind(value_rows, "cam", -1)
    marked = mark(valid_count, key_rows)
    lower_keys = from_behind(marked, "cam", 1)
    upper_keys = from_behind(marked, "cam", -1)
    packed = pack(query_rows, marked, value_rows, grad_rows, frames)
    rows = packed.shape[3]
    arrived = exchange(packed.reshape(frames, 4 * rows, PAIR))
    cross_out, cross_query, own_grads, lower_grads, upper_grads = cross(
        query_rows,
        grad_rows,
        (lower_keys, marked, upper_keys),
        (lower_values, value_rows, upper_values),
    )
    from_upper = from_behind(lower_grads, "cam", -1)
    from_lower = from_behind(upper_grads, "cam", 1)
    arrived, cross_out = lax.optimization_barrier((arrived, cross_out))
    answered = temporal(arrived.reshape(frames, 4, rows, PAIR))
    returned = exchange(answered.reshape(frames, 4 * rows, PAIR)).reshape(packed.shape)
    key_total, value_total = total(own_grads, from_upper, from_lower)
    results = finish(returned, cross_out, cross_query, key_total, value_total)
    return tuple(result[None, None] for result in results)


def solution(mesh):
    placed = (
        P("cam", "frame", None, None),
        P("cam", "frame", None, None),
        P("cam", "frame", None, None),
        P("cam", "frame", None, None),
        P("cam", "frame"),
    )
    return jax.shard_map(
        on_device,
        mesh=mesh,
        in_specs=placed,
        out_specs=(
            P("cam", "frame", None, None),
            P("cam", "frame", None, None),
            P("cam", "frame", None, None),
            P("cam", "frame", None, None),
        ),
        check_vma=False,
    )
```

```python
import jax
import jax.numpy as jnp
from jax import lax
from jax.experimental import pallas as pl
from jax.experimental.pallas import tpu as pltpu
from jax.sharding import PartitionSpec as P

HEAD_DIM = 64
PAIR = 128
MARK = 1024.0
MARK_CUT = 512.0
MASKED = -1e30
SCALE = HEAD_DIM ** (-0.5)
ROW_T = (((1,), (1,)), ((), ()))
VMEM_BYTES = 60 * 1024 * 1024
ROOMY_BYTES = 24 * 1024 * 1024


def contract(left, right, dims):
    return lax.dot_general(left, right, dims, preferred_element_type=jnp.float32)


def multiply(left, right):
    return jnp.dot(left, right, preferred_element_type=jnp.float32)


def params(limit=VMEM_BYTES):
    return pltpu.CompilerParams(vmem_limit_bytes=limit)


def mark_kernel(count_ref, k_ref, marked_ref):
    positions = lax.broadcasted_iota(jnp.int32, k_ref.shape, 0) + pl.program_id(0) * k_ref.shape[0]
    wide = k_ref[...].astype(jnp.float32)
    marked_ref[...] = jnp.where(positions < count_ref[0, 0], wide, MARK).astype(jnp.bfloat16)


def mark(count, keys):
    length, width = keys.shape
    row_spec = pl.BlockSpec((length // 2, width), lambda i: (i, 0))
    return pl.pallas_call(
        mark_kernel,
        grid=(2,),
        in_specs=[pl.BlockSpec(memory_space=pltpu.SMEM), row_spec],
        out_specs=row_spec,
        out_shape=jax.ShapeDtypeStruct(keys.shape, jnp.bfloat16),
        compiler_params=params(),
        cost_estimate=pl.CostEstimate(
            flops=length * width, bytes_accessed=4 * length * width, transcendentals=0
        ),
        name="mark",
    )(count, keys)


def pack_kernel(*refs):
    x_ref = refs[-1]
    blocks, pairs, _, rows, _ = x_ref.shape
    for index, ref in enumerate(refs[:-1]):
        for pair in range(pairs):
            part = ref[:, pair * PAIR : (pair + 1) * PAIR]
            x_ref[:, pair, index] = part.reshape(blocks, rows, PAIR)


def pack(queries, keys, values, cotangents, frames):
    length, width = queries.shape
    pairs = width // PAIR
    blocks = frames // pairs
    rows = length // blocks
    per_step = 4
    row_spec = pl.BlockSpec((per_step * rows, width), lambda i: (i, 0))
    return pl.pallas_call(
        pack_kernel,
        grid=(blocks // per_step,),
        in_specs=[row_spec] * 4,
        out_specs=pl.BlockSpec((per_step, pairs, 4, rows, PAIR), lambda i: (i, 0, 0, 0, 0)),
        out_shape=jax.ShapeDtypeStruct((blocks, pairs, 4, rows, PAIR), jnp.bfloat16),
        compiler_params=params(),
        cost_estimate=pl.CostEstimate(
            flops=length * width, bytes_accessed=16 * length * width, transcendentals=0
        ),
        name="pack",
    )(queries, keys, values, cotangents)


def cross_kernel(q_ref, g_ref, *refs):
    key_refs, value_refs = refs[:3], refs[3:6]
    o_ref, dq_ref, own_out, low_out, up_out = refs[6:]
    length = q_ref.shape[0]
    first = lax.broadcasted_iota(jnp.int32, (length, PAIR), 1) < HEAD_DIM
    marked = jnp.concatenate([ref[...] for ref in key_refs], axis=0)
    values = jnp.concatenate([ref[...] for ref in value_refs], axis=0)
    wide = marked.astype(jnp.float32)
    invalid = wide > MARK_CUT
    keys_wide = jnp.where(invalid, 0.0, wide)
    keys = keys_wide.astype(jnp.bfloat16)
    bias = jnp.where(invalid, MASKED, 0.0)
    bias = jnp.concatenate([bias] * (length // PAIR), axis=1)
    keys_t = keys_wide.T.astype(jnp.bfloat16)
    values_t = values.astype(jnp.float32).T.astype(jnp.bfloat16)
    queries = q_ref[...].astype(jnp.float32) * SCALE
    cotangents = g_ref[...].astype(jnp.float32)
    outputs = []
    query_grads = []
    key_grad = None
    value_grad = None
    for head in range(PAIR // HEAD_DIM):
        mine = first if head == 0 else jnp.logical_not(first)
        query = jnp.where(mine, queries, 0.0).astype(jnp.bfloat16)
        cotangent = jnp.where(mine, cotangents, 0.0).astype(jnp.bfloat16)
        scores = contract(keys, query, ROW_T) + bias
        shifted = jnp.exp(scores - jnp.max(scores, axis=0, keepdims=True))
        probs = shifted * (1.0 / jnp.sum(shifted, axis=0, keepdims=True))
        probs_low = probs.astype(jnp.bfloat16)
        grad_probs = contract(values, cotangent, ROW_T)
        row_delta = jnp.sum(probs * grad_probs, axis=0, keepdims=True)
        grad_scores = (probs * (grad_probs - row_delta)).astype(jnp.bfloat16)
        rows = slice(head * HEAD_DIM, (head + 1) * HEAD_DIM)
        outputs.append(multiply(values_t[rows], probs_low))
        query_grads.append(multiply(keys_t[rows], grad_scores))
        value_part = multiply(probs_low, cotangent)
        key_part = multiply(grad_scores, query)
        key_grad = key_part if head == 0 else key_grad + key_part
        value_grad = value_part if head == 0 else value_grad + value_part
    o_ref[...] = jnp.concatenate(outputs, axis=0).T.astype(jnp.bfloat16)
    dq_ref[...] = (jnp.concatenate(query_grads, axis=0).T * SCALE).astype(jnp.bfloat16)
    for index, grad in enumerate((key_grad, value_grad)):
        low_out[0, index] = grad[:length].astype(jnp.bfloat16)
        own_out[0, index] = grad[length : 2 * length]
        up_out[0, index] = grad[2 * length :].astype(jnp.bfloat16)


def cross(queries, cotangents, keys, values):
    length, width = queries.shape
    pairs = width // PAIR
    column_spec = pl.BlockSpec((length, PAIR), lambda j: (0, j))
    pair_spec = pl.BlockSpec((1, 2, length, PAIR), lambda j: (j, 0, 0, 0))
    flat = jax.ShapeDtypeStruct((length, width), jnp.bfloat16)
    paired = jax.ShapeDtypeStruct((pairs, 2, length, PAIR), jnp.float32)
    paired_low = jax.ShapeDtypeStruct((pairs, 2, length, PAIR), jnp.bfloat16)
    return pl.pallas_call(
        cross_kernel,
        grid=(pairs,),
        in_specs=[column_spec] * 8,
        out_specs=[column_spec] * 2 + [pair_spec] * 3,
        out_shape=[flat, flat, paired, paired_low, paired_low],
        compiler_params=params(),
        cost_estimate=pl.CostEstimate(
            flops=10000 * length * length * width,
            bytes_accessed=24 * length * width * 2,
            transcendentals=48 * length * length,
        ),
        name="cross_view",
    )(queries, cotangents, *keys, *values)


def temporal_kernel(y_ref, z_ref):
    frames, _, positions, _ = y_ref.shape
    first = lax.broadcasted_iota(jnp.int32, (frames, PAIR), 1) < HEAD_DIM
    rows_in = [jnp.swapaxes(y_ref[:, index].astype(jnp.float32), 0, 1) for index in range(4)]
    rows_out = [[], [], [], []]

    def stacked(rows):
        return jnp.concatenate(
            [jnp.where(first, rows, 0.0), jnp.where(first, 0.0, rows)], axis=0
        ).astype(jnp.bfloat16)

    def diagonal(full):
        return jnp.where(first, full[:frames], full[frames:])

    group = 8
    for start in range(0, positions, group):
        held = []
        for position in range(start, start + group):
            marked = rows_in[1][position]
            invalid = marked > MARK_CUT
            keys = jnp.where(invalid, 0.0, marked).astype(jnp.bfloat16)
            values = rows_in[2][position].astype(jnp.bfloat16)
            queries = stacked(rows_in[0][position] * SCALE)
            cotangents = stacked(rows_in[3][position])
            scores = jnp.where(invalid, MASKED, contract(keys, queries, ROW_T))
            grad_probs = contract(values, cotangents, ROW_T)
            held.append((keys, values, queries, cotangents, scores, grad_probs))
        for keys, values, queries, cotangents, scores, grad_probs in held:
            shifted = jnp.exp(scores - jnp.max(scores, axis=0, keepdims=True))
            probs = shifted * (1.0 / jnp.sum(shifted, axis=0, keepdims=True))
            row_delta = jnp.sum(probs * grad_probs, axis=0, keepdims=True)
            grad_scores = probs * (grad_probs - row_delta)
            rows_out[0].append(diagonal(multiply(probs.T.astype(jnp.bfloat16), values)))
            query_part = diagonal(multiply(grad_scores.T.astype(jnp.bfloat16), keys))
            rows_out[1].append(query_part * SCALE)
            rows_out[2].append(multiply(grad_scores.astype(jnp.bfloat16), queries))
            rows_out[3].append(multiply(probs.astype(jnp.bfloat16), cotangents))
    for index in range(4):
        z_ref[:, index] = jnp.swapaxes(jnp.stack(rows_out[index]), 0, 1).astype(jnp.bfloat16)


def temporal(blocks):
    frames, _, positions, _ = blocks.shape
    per_step = 16
    spec = pl.BlockSpec((frames, 4, per_step, PAIR), lambda i: (0, 0, i, 0))
    return pl.pallas_call(
        temporal_kernel,
        grid=(positions // per_step,),
        in_specs=[spec],
        out_specs=spec,
        out_shape=pltpu.HBM(blocks.shape, jnp.bfloat16),
        compiler_params=params(ROOMY_BYTES),
        cost_estimate=pl.CostEstimate(
            flops=12 * positions * frames * frames * PAIR,
            bytes_accessed=4 * blocks.size,
            transcendentals=2 * positions * frames * frames,
        ),
        name="temporal",
    )(blocks)


def total_kernel(own_ref, low_ref, up_ref, key_ref, value_ref):
    for pair in range(own_ref.shape[0]):
        columns = slice(pair * PAIR, (pair + 1) * PAIR)
        for index, total_ref in enumerate((key_ref, value_ref)):
            total_ref[:, columns] = (
                own_ref[pair, index]
                + low_ref[pair, index].astype(jnp.float32)
                + up_ref[pair, index].astype(jnp.float32)
            ).astype(jnp.bfloat16)


def total(own, lower, upper):
    pairs, _, length, _ = own.shape
    per_step = 2
    pair_spec = pl.BlockSpec((per_step, 2, length, PAIR), lambda j: (j, 0, 0, 0))
    return pl.pallas_call(
        total_kernel,
        grid=(pairs // per_step,),
        in_specs=[pair_spec] * 3,
        out_specs=[pl.BlockSpec((length, per_step * PAIR), lambda j: (0, j))] * 2,
        out_shape=[jax.ShapeDtypeStruct((length, pairs * PAIR), jnp.bfloat16)] * 2,
        compiler_params=params(),
        cost_estimate=pl.CostEstimate(
            flops=10**12,
            bytes_accessed=12 * own.size,
            transcendentals=0,
        ),
        name="total",
    )(own, lower, upper)


def finish_kernel(w_ref, *refs):
    cross_refs, out_refs = refs[:4], refs[4:]
    height = cross_refs[0].shape[0]
    for pair in range(w_ref.shape[1]):
        columns = slice(pair * PAIR, (pair + 1) * PAIR)
        for index, (cross_ref, out_ref) in enumerate(zip(cross_refs, out_refs)):
            returned = w_ref[:, pair, index].reshape(height, PAIR).astype(jnp.float32)
            crossed = cross_ref[:, columns].astype(jnp.float32)
            out_ref[:, columns] = (crossed + returned).astype(jnp.bfloat16)


def finish(returned, *cross_parts):
    length, width = cross_parts[0].shape
    blocks, pairs, _, rows, _ = returned.shape
    per_step = 4
    row_spec = pl.BlockSpec((per_step * rows, width), lambda i: (i, 0))
    return pl.pallas_call(
        finish_kernel,
        grid=(blocks // per_step,),
        in_specs=[pl.BlockSpec((per_step, pairs, 4, rows, PAIR), lambda i: (i, 0, 0, 0, 0))]
        + [row_spec] * 4,
        out_specs=[row_spec] * 4,
        out_shape=[jax.ShapeDtypeStruct((length, width), jnp.bfloat16)] * 4,
        compiler_params=params(ROOMY_BYTES),
        cost_estimate=pl.CostEstimate(
            flops=4 * length * width, bytes_accessed=32 * length * width, transcendentals=0
        ),
        name="finish",
    )(returned, *(pltpu.with_memory_space_constraint(part, pltpu.HBM) for part in cross_parts))


def from_behind(shard, axis, by):
    devices = lax.axis_size(axis)
    return lax.ppermute(shard, axis, [(i, (i + by) % devices) for i in range(devices)])


def exchange(blocks):
    return lax.all_to_all(blocks, "frame", split_axis=0, concat_axis=0, tiled=True)


def on_device(queries, key_vectors, value_vectors, out_grad, valid_count):
    query_rows = queries[0, 0]
    key_rows = key_vectors[0, 0]
    value_rows = value_vectors[0, 0]
    grad_rows = out_grad[0, 0]
    frames = lax.axis_size("frame")
    lower_values = from_behind(value_rows, "cam", 1)
    upper_values = from_behind(value_rows, "cam", -1)
    marked = mark(valid_count, key_rows)
    lower_keys = from_behind(marked, "cam", 1)
    upper_keys = from_behind(marked, "cam", -1)
    packed = pack(query_rows, marked, value_rows, grad_rows, frames)
    rows = packed.shape[3]
    arrived = exchange(packed.reshape(frames, 4 * rows, PAIR))
    cross_out, cross_query, own_grads, lower_grads, upper_grads = cross(
        query_rows,
        grad_rows,
        (lower_keys, marked, upper_keys),
        (lower_values, value_rows, upper_values),
    )
    from_upper = from_behind(lower_grads, "cam", -1)
    from_lower = from_behind(upper_grads, "cam", 1)
    arrived, cross_out = lax.optimization_barrier((arrived, cross_out))
    answered = temporal(arrived.reshape(frames, 4, rows, PAIR))
    returned = exchange(answered.reshape(frames, 4 * rows, PAIR)).reshape(packed.shape)
    key_total, value_total = total(own_grads, from_upper, from_lower)
    results = finish(returned, cross_out, cross_query, key_total, value_total)
    return tuple(result[None, None] for result in results)


def solution(mesh):
    placed = (
        P("cam", "frame", None, None),
        P("cam", "frame", None, None),
        P("cam", "frame", None, None),
        P("cam", "frame", None, None),
        P("cam", "frame"),
    )
    return jax.shard_map(
        on_device,
        mesh=mesh,
        in_specs=placed,
        out_specs=(
            P("cam", "frame", None, None),
            P("cam", "frame", None, None),
            P("cam", "frame", None, None),
            P("cam", "frame", None, None),
        ),
        check_vma=False,
    )
```
